256 devices in a mesh: tile: 16 (over y, z_hi, core), band: 16 (over z_lo, x).
Axes of the slice: x: 4, y: 4, z: 8 (z_hi: 2, z_lo: 4; z = z_hi * 4 + z_lo), core: 2. Of those that a mesh axis runs over, the one named last changes fastest.
Arguments:
- features: bfloat16 [1024, 96, 512], P(('tile', 'band')), may hold values from -6 to 6
- occupancy: int32 [1024, 512], P(('tile', 'band')), may hold values 0 or 1
- weights: bfloat16 [27, 96, 96], replicated, may hold values from -0.125 to 0.125
- grad_out: bfloat16 [1024, 96, 512], P(('tile', 'band')), may hold values from -6 to 6
- lat_src: int32 [1024, 4], P(('tile', 'band')), may hold values from -1 to 23, as said below
- down_src: int32 [1024], P(('tile', 'band')), may hold values from -1 to 3, as said below
- up_src: int32 [1024], P(('tile', 'band')), may hold values from -1 to 3, as said below
- send_faces: int32 [256, 4, 2], P(('tile', 'band')), may hold values from 0 to 15, as said below
Outputs:
- layer_out: bfloat16 [1024, 96, 512], P(('tile', 'band'))
- input_grad: bfloat16 [1024, 96, 512], P(('tile', 'band'))
- weight_grad: float32 [27, 96, 96], replicated
The draws below stay inside these ranges and needn't reach their ends.
Inputs may be any that keep to these rules, and one draw needn't show every extreme that they name: `lat_src`: neighbour relations are mutual: a block's side slab comes from the block whose opposite side takes this block's face. A cross-tile neighbour of a block in tile t lies in tile t XOR 2^k for some round k, and in round k every device sends exactly 2 faces to that tile, the ones that tile's entries name. `send_faces`: entries are codes f * 4 + j of face f < 4 of local block j. `down_src`: mutual with up_src; -1 in the lowest band. `up_src`: mutual with down_src; -1 in the highest band.
All inputs are finite; a program needn't handle non-finite values. No bound on the sum of `occupancy` on one device may be relied on, other than what follows from the above.
Results may differ from the reference program's by a relative error of at most 0.0029.
Values may be sent and summed in bfloat16 or wider, within the bound.
No kernel may reach another device: no remote copies, remote signals or barrier semaphores. Data moves between devices by JAX's collectives and lax.ppermute only.
A program may use at most 128 MiB of HBM per device.

```python
import math
import jax
import jax.numpy as jnp
from jax import lax

CHANNELS = 96
BLOCK_DEV = 4
LINKS = 2
ROUNDS = 4
BLOCKS = 1024
N_TILE = 16
N_BAND = 16


def shuffled(key, shape):
    scores = jax.random.randint(key, shape, 0, 1 << 20) * shape[-1] + jnp.arange(shape[-1], dtype=jnp.int32)
    return jnp.argsort(scores, axis=-1).astype(jnp.int32)


def side_sources(rank, partner_perm, keep, axis_index, tile_index, block_ids, wanted_bit, partner_code):
    bit_index = 2 * (rank // LINKS) + axis_index
    crossing = bit_index < ROUNDS
    tile_bit = jnp.right_shift(tile_index, jnp.minimum(bit_index, ROUNDS - 1)) % 2
    partner_block = jnp.take_along_axis(partner_perm, rank, axis=-1)
    kept = jnp.take_along_axis(keep, rank, axis=-1) & (partner_block != block_ids)
    remote = jnp.where(tile_bit == wanted_bit, 4 * BLOCK_DEV + bit_index * LINKS + rank % LINKS, -1)
    inside = jnp.where(kept, partner_code * BLOCK_DEV + partner_block, -1)
    return jnp.where(crossing, remote, inside).astype(jnp.int32)


def geometry(key):
    shape = (N_TILE, N_BAND, 2, BLOCK_DEV)
    plus_perm = shuffled(jax.random.fold_in(key, 11), shape)
    minus_perm = shuffled(jax.random.fold_in(key, 12), shape)
    plus_rank = jnp.argsort(plus_perm, axis=-1).astype(jnp.int32)
    minus_rank = jnp.argsort(minus_perm, axis=-1).astype(jnp.int32)
    keep = jax.random.randint(jax.random.fold_in(key, 13), shape, 0, 4) > 0
    tile_index = jnp.arange(N_TILE, dtype=jnp.int32)[:, None, None, None]
    axis_index = jnp.arange(2, dtype=jnp.int32)[None, None, :, None]
    block_ids = jnp.arange(BLOCK_DEV, dtype=jnp.int32)
    plus_src = side_sources(plus_rank, minus_perm, keep, axis_index, tile_index, block_ids, 0, 2 * axis_index)
    minus_src = side_sources(minus_rank, plus_perm, keep, axis_index, tile_index, block_ids, 1, 2 * axis_index + 1)
    lateral = jnp.stack([minus_src[:, :, 0], plus_src[:, :, 0], minus_src[:, :, 1], plus_src[:, :, 1]], axis=-1)
    round_ids = jnp.arange(ROUNDS, dtype=jnp.int32)[:, None]
    link_ids = jnp.arange(LINKS, dtype=jnp.int32)[None, :]
    axis_of = round_ids % 2 + 0 * link_ids
    rank_of = round_ids // 2 * LINKS + link_ids
    tile_bits = jnp.right_shift(jnp.arange(N_TILE, dtype=jnp.int32)[:, None, None, None], round_ids[None, None]) % 2
    plus_pick = plus_perm[:, :, axis_of, rank_of]
    minus_pick = minus_perm[:, :, axis_of, rank_of]
    sends = jnp.where(tile_bits == 0, (2 * axis_of + 1) * BLOCK_DEV + plus_pick, 2 * axis_of * BLOCK_DEV + minus_pick)
    up_perm = shuffled(jax.random.fold_in(key, 14), (N_TILE, N_BAND, BLOCK_DEV))
    up_rank = jnp.argsort(up_perm, axis=-1).astype(jnp.int32)
    keep_up = jax.random.randint(jax.random.fold_in(key, 15), (N_TILE, N_BAND, BLOCK_DEV), 0, 4) > 0
    band_ids = jnp.arange(N_BAND, dtype=jnp.int32)[None, :, None]
    up_src = jnp.where(keep_up & (band_ids < N_BAND - 1), up_perm, -1)
    prev_rank = jnp.roll(up_rank, 1, axis=1)
    prev_keep = jnp.take_along_axis(jnp.roll(keep_up, 1, axis=1), prev_rank, axis=-1)
    down_src = jnp.where(prev_keep & (band_ids > 0), prev_rank, -1)
    return (lateral.reshape(BLOCKS, 4).astype(jnp.int32), down_src.reshape(BLOCKS).astype(jnp.int32), up_src.reshape(BLOCKS).astype(jnp.int32), sends.reshape(N_TILE * N_BAND, ROUNDS, LINKS).astype(jnp.int32))


def draw_lat_src(key, part):
    return geometry(key)[0]


def draw_down_src(key, part):
    return geometry(key)[1]


def draw_up_src(key, part):
    return geometry(key)[2]


def draw_send_faces(key, part):
    return geometry(key)[3]


def plant(values, stream_key, smallest, top_value):
    longest = values.shape.index(max(values.shape))
    spots = []
    for shift in (0, 1):
        where = [jax.random.randint(jax.random.fold_in(stream_key, axis), (), 0, length) for axis, length in enumerate(values.shape)]
        where[longest] = (where[longest] + shift) % values.shape[longest]
        spots.append(tuple(where))
    return values.at[spots[0]].set(smallest).at[spots[1]].set(top_value)


def steps_of(own_key, dims, cuts, least, high):
    def one(axis_at, parts):
        draws = jax.random.uniform(jax.random.fold_in(jax.random.fold_in(own_key, 6), axis_at), (parts,), jnp.float32, least / len(cuts), high / len(cuts))
        return jnp.repeat(jnp.exp(draws), dims[axis_at] // parts).reshape((-1,) + (1,) * (len(dims) - axis_at - 1))

    factor_of = one(*cuts[0])
    for cut in cuts[1:]:
        factor_of = factor_of * one(*cut)
    return factor_of


def centred(rng, shape, scale, reach, cuts=(), held_as=jnp.bfloat16):
    gain = steps_of(rng, shape, cuts, -0.22, 0.18) if cuts else 1.0
    entries = jax.random.normal(rng, shape, jnp.float32) * scale * gain
    return jnp.minimum(jnp.maximum(entries, -reach), reach).astype(held_as)


def setup_inputs(seed: int = 0) -> dict:
    seeds = jax.random.split(jax.random.key(seed), 9)
    return {
        "features": centred(seeds[0], (BLOCKS, CHANNELS, 512), 1.0, 6.0, ((0, 256),)),
        "occupancy": plant((jax.random.randint(seeds[1], (BLOCKS, 512), 0, 3) < 2).astype(jnp.int32), jax.random.fold_in(seeds[1], 1), 0, 1),
        "weights": centred(seeds[2], (27, CHANNELS, CHANNELS), (27 * CHANNELS) ** -0.5, 0.125),
        "grad_out": centred(seeds[3], (BLOCKS, CHANNELS, 512), 1.0, 6.0, ((0, 256),)),
        "lat_src": draw_lat_src(jax.random.fold_in(seeds[8], 71), 0),
        "down_src": draw_down_src(jax.random.fold_in(seeds[8], 71), 0),
        "up_src": draw_up_src(jax.random.fold_in(seeds[8], 71), 0),
        "send_faces": draw_send_faces(jax.random.fold_in(seeds[8], 71), 0),
    }


def cube_faces(cube_data):
    num_blocks, channels = (cube_data.shape[0], cube_data.shape[1])
    layers = [cube_data[:, :, 0], cube_data[:, :, 7], cube_data[:, :, :, 0], cube_data[:, :, :, 7], cube_data[:, :, :, :, 0], cube_data[:, :, :, :, 7]]
    return jnp.stack([layer.reshape(num_blocks, channels, 64) for layer in layers])

def pad_cube(cube_data, slabs):
    num_blocks, channels = (cube_data.shape[0], cube_data.shape[1])
    square = slabs.reshape(6, num_blocks, channels, 8, 8)
    padded = jnp.pad(cube_data, ((0, 0), (0, 0), (1, 1), (1, 1), (1, 1)))
    padded = padded.at[:, :, 0, 1:9, 1:9].set(square[0])
    padded = padded.at[:, :, 9, 1:9, 1:9].set(square[1])
    padded = padded.at[:, :, 1:9, 0, 1:9].set(square[2])
    padded = padded.at[:, :, 1:9, 9, 1:9].set(square[3])
    padded = padded.at[:, :, 1:9, 1:9, 0].set(square[4])
    padded = padded.at[:, :, 1:9, 1:9, 9].set(square[5])
    return padded

def tap_slab(padded, group_index):
    shift_x, shift_y = (group_index // 3, group_index % 3)
    num_blocks, channels = (padded.shape[0], padded.shape[1])
    pieces = [padded[:, :, shift_x:shift_x + 8, shift_y:shift_y + 8, shift_z:shift_z + 8].reshape(num_blocks, channels, 512) for shift_z in range(3)]
    return jnp.concatenate(pieces, axis=1)

def convolve(padded, weights):
    num_blocks, channels = (padded.shape[0], padded.shape[1])
    outputs = weights.shape[2]
    running = jnp.zeros((num_blocks, outputs, 512), jnp.float32)
    for group_index in range(9):
        tap_rows = tap_slab(padded, group_index).astype(jnp.float32)
        matrix = weights[3 * group_index:3 * group_index + 3].reshape(3 * channels, outputs).astype(jnp.float32)
        running = running + jnp.einsum('bkv,ko->bov', tap_rows, matrix)
    return running

def group_term(padded, delta_grad, group_index):
    tap_rows = tap_slab(padded, group_index).astype(jnp.float32)
    channels = padded.shape[1]
    term = jnp.einsum('bkv,bov->ko', tap_rows, delta_grad.astype(jnp.float32))
    return term.reshape(3, channels, delta_grad.shape[1])

def gather_slabs(cube_data, lat_src, down_src, up_src, send_faces):
    face_set = cube_faces(cube_data)
    total_blocks = cube_data.shape[0]
    block_ids = jnp.arange(total_blocks, dtype=jnp.int32)
    device = block_ids // BLOCK_DEV
    tile_index = device // N_BAND
    band_index = device % N_BAND
    own_limit = 4 * BLOCK_DEV
    remote_offset = lat_src - own_limit
    round_index = jnp.clip(remote_offset // LINKS, 0, ROUNDS - 1).astype(jnp.int32)
    slot_index = (remote_offset % LINKS).astype(jnp.int32)
    partner_tile = jnp.bitwise_xor(tile_index[:, None], jnp.left_shift(jnp.int32(1), round_index))
    remote_dev = (partner_tile * N_BAND + band_index[:, None]).astype(jnp.int32)
    remote_code = send_faces[remote_dev, round_index, slot_index]
    is_local = lat_src < own_limit
    face_code = jnp.where(is_local, jnp.clip(lat_src, 0, own_limit - 1), remote_code)
    source_dev = jnp.where(is_local, device[:, None], remote_dev)
    source_block = (source_dev * BLOCK_DEV + face_code % BLOCK_DEV).astype(jnp.int32)
    lateral = face_set[face_code // BLOCK_DEV, source_block]
    lateral = jnp.where((lat_src >= 0)[:, :, None, None], lateral, jnp.zeros_like(lateral))
    down_valid = (down_src >= 0) & (band_index > 0)
    down_block = jnp.clip((device - 1) * BLOCK_DEV + down_src, 0, total_blocks - 1).astype(jnp.int32)
    down_slab = face_set[5][down_block]
    down_slab = jnp.where(down_valid[:, None, None], down_slab, jnp.zeros_like(down_slab))
    up_valid = (up_src >= 0) & (band_index < N_BAND - 1)
    up_block = jnp.clip((device + 1) * BLOCK_DEV + up_src, 0, total_blocks - 1).astype(jnp.int32)
    up_slab = face_set[4][up_block]
    up_slab = jnp.where(up_valid[:, None, None], up_slab, jnp.zeros_like(up_slab))
    return jnp.concatenate([lateral.transpose(1, 0, 2, 3), down_slab[None], up_slab[None]])

def run_conv(padded, weights):
    shaped = padded.reshape((padded.shape[0] // BLOCK_DEV, BLOCK_DEV) + padded.shape[1:])
    result = lax.map(lambda device_piece: convolve(device_piece, weights), shaped)
    return result.reshape((padded.shape[0],) + result.shape[2:])

def weight_sum(padded, delta_grad):
    devices = padded.shape[0] // BLOCK_DEV
    shaped_pad = padded.reshape((devices, BLOCK_DEV) + padded.shape[1:])
    shaped_delta = delta_grad.reshape((devices, BLOCK_DEV) + delta_grad.shape[1:])

    def add_device(running, pieces):
        terms = [group_term(pieces[0], pieces[1], group_index) for group_index in range(9)]
        return (running + jnp.concatenate(terms), None)
    initial = jnp.zeros((27, CHANNELS, CHANNELS), jnp.float32)
    result, unused = lax.scan(add_device, initial, (shaped_pad, shaped_delta))
    return result

def reference(features, occupancy, weights, grad_out, lat_src, down_src, up_src, send_faces):
    total_blocks = features.shape[0]
    mask_float = occupancy.astype(jnp.float32)[:, None, :]
    masked = features * occupancy.astype(jnp.bfloat16)[:, None, :]
    cube_data = masked.reshape(total_blocks, CHANNELS, 8, 8, 8)
    padded = pad_cube(cube_data, gather_slabs(cube_data, lat_src, down_src, up_src, send_faces))
    preact = run_conv(padded, weights)
    sigmoid_value = jax.nn.sigmoid(preact)
    layer_out = (features.astype(jnp.float32) + mask_float * (preact * sigmoid_value)).astype(jnp.bfloat16)
    delta_grad = (grad_out.astype(jnp.float32) * mask_float * (sigmoid_value * (1.0 + preact * (1.0 - sigmoid_value)))).astype(jnp.bfloat16)
    delta_cube = delta_grad.reshape(total_blocks, CHANNELS, 8, 8, 8)
    delta_padded = pad_cube(delta_cube, gather_slabs(delta_cube, lat_src, down_src, up_src, send_faces))
    flipped = jnp.flip(weights, 0).transpose(0, 2, 1)
    back_term = run_conv(delta_padded, flipped)
    input_grad = (grad_out.astype(jnp.float32) + mask_float * back_term).astype(jnp.bfloat16)
    weight_grad = weight_sum(padded, delta_grad) * (1.0 / math.sqrt(BLOCKS * 512))
    return (layer_out, input_grad, weight_grad)
```

```python
import functools
import math

import jax
import jax.numpy as jnp
import numpy as np
from jax import lax
from jax.experimental import pallas as pl
from jax.experimental.pallas import tpu as pltpu
from jax.sharding import Mesh
from jax.sharding import PartitionSpec as P

NB, C, V, TAPS = 4, 96, 512, 27
BF16, F32 = jnp.bfloat16, jnp.float32
TILE = ("y", "zh", "c")
BAND = ("zl", "x")
EVERY = TILE + BAND
PLANE = ("y", "x")
COLUMN = ("zh", "zl")
ROWS, HALF = 2048, 1024
SCALE = 1.0 / math.sqrt(1024 * 512)
SHIFTS = [(dy, dz) for dy in range(3) for dz in range(3)]
VMEM_LIMIT = 56 * 1024 * 1024


def face_matrix():
    table = np.zeros((V, 6 * 128), np.float32)
    for f in range(6):
        for a in range(8):
            for b in range(8):
                if f < 2:
                    v = 448 * f + 8 * a + b
                elif f < 4:
                    v = 64 * a + 56 * (f - 2) + b
                else:
                    v = 64 * a + 8 * b + 7 * (f - 4)
                table[v, 128 * f + 8 * a + b] = 1
                table[v, 128 * f + 64 + 8 * a + b] = 1
    return table


def halo_matrix():
    table = np.zeros((256, 9, V), np.float32)
    for t, (dy, dz) in enumerate(SHIFTS):
        for v in range(V):
            x, y, z = v // 64, v // 8 % 8 + dy - 1, v % 8 + dz - 1
            in_y, in_z = 0 <= y < 8, 0 <= z < 8
            if in_z and not in_y:
                table[(0 if y < 0 else 64) + 8 * x + z, t, v] = 1
            elif in_y and not in_z:
                table[(128 if z < 0 else 192) + 8 * x + y, t, v] = 1
    return table.reshape(256, 9 * V)


def lane_low(rows):
    return lax.broadcasted_iota(jnp.int32, (rows, 128), 1) < 64


def write_faces(data, pf, send_ref, own_ref, lat_ref, zf_ref):
    flat = data.reshape(NB * C, V)
    faces = jnp.dot(flat, pf, preferred_element_type=F32).astype(BF16)
    low = lane_low(C)
    for f in range(4):
        for b in range(NB):
            own_ref[NB * f + b] = faces[C * b : C * (b + 1), 128 * f : 128 * (f + 1)]
    for d in range(2):
        for h in range(2):
            cols = slice(128 * (4 + d), 128 * (5 + d))
            first = faces[C * 2 * h : C * (2 * h + 1), cols]
            second = faces[C * (2 * h + 1) : C * (2 * h + 2), cols]
            zf_ref[d, h] = jnp.where(low, first, second)
    for k in range(4):
        lat_ref[k] = jnp.where(low, own_ref[send_ref[0, k, 0]], own_ref[send_ref[0, k, 1]])


def fill_pool(own_ref, recv_ref, down_ref, up_ref, pool):
    low = lane_low(C)

    def spread(pair, at):
        turned = pltpu.roll(pair, 64, 1)
        pool[at] = jnp.where(low, pair, turned)
        pool[at + 1] = jnp.where(low, turned, pair)

    zero = jnp.zeros((C, 128), BF16)
    for i in range(16):
        pool[i] = own_ref[i]
    for k in range(4):
        spread(recv_ref[k], 16 + 2 * k)
    pool[24] = zero
    for h in range(2):
        spread(down_ref[h], 25 + 2 * h)
        spread(up_ref[h], 30 + 2 * h)
    pool[29] = zero
    pool[34] = zero


def build_taps(data, pool, src_ref, down_ref, up_ref, e_ref, slabs, halo, x_ref):
    low = lane_low(C)
    side_x = []
    for b in range(NB):
        lat = [pool[jnp.where(src_ref[b, i] < 0, 24, src_ref[b, i])] for i in range(4)]
        below = pool[jnp.where(down_ref[b] < 0, 29, 25 + down_ref[b])]
        above = pool[jnp.where(up_ref[b] < 0, 34, 30 + up_ref[b])]
        side_x.append(jnp.where(low, lat[0], lat[1]))
        slabs[C * b : C * (b + 1), 0:128] = jnp.where(low, lat[2], lat[3])
        slabs[C * b : C * (b + 1), 128:256] = jnp.where(low, below, above)
    lanes = lax.broadcasted_iota(jnp.int32, (C, V), 1)
    lane_y, lane_z = (lanes >> 3) & 7, lanes & 7
    for t, (dy, dz) in enumerate(SHIFTS):
        step = 8 * (dy - 1) + dz - 1
        if step:
            halo[...] = jnp.dot(
                slabs[...], e_ref[:, V * t : V * (t + 1)], preferred_element_type=F32
            ).astype(BF16)
            at_y, at_z = lane_y + (dy - 1), lane_z + (dz - 1)
            inside = (at_y >= 0) & (at_y < 8) & (at_z >= 0) & (at_z < 8)
        for b in range(NB):
            if step:
                shifted = pltpu.roll(data[b], (-step) % V, 1)
                shifted = jnp.where(inside, shifted, halo[C * b : C * (b + 1), :])
                edge = pltpu.roll(side_x[b], (-step) % 128, 1)
                edge = jnp.where(inside[:, :128], edge, jnp.zeros_like(edge))
            else:
                shifted, edge = data[b], side_x[b]
            turned = [pltpu.roll(shifted[:, 128 * i : 128 * (i + 1)], 64, 1) for i in range(4)]
            between = [jnp.where(low, turned[i], turned[i + 1]) for i in range(3)]
            columns = [jnp.where(low, edge, turned[0])] + between + [jnp.where(low, turned[3], edge)]
            at = [C * (9 * dx + t) for dx in range(3)]
            x_ref[at[1] : at[1] + C, V * b : V * (b + 1)] = shifted
            for i in range(4):
                place = slice(V * b + 128 * i, V * b + 128 * (i + 1))
                x_ref[at[0] : at[0] + C, place] = columns[i]
                x_ref[at[2] : at[2] + C, place] = columns[i + 1]


def masked_of(feat_ref, occ_ref):
    return feat_ref[...] * occ_ref[...].astype(F32).astype(BF16)


def faces_kernel(feat_ref, occ_ref, pf_ref, send_ref, own_ref, lat_ref, zf_ref):
    write_faces(masked_of(feat_ref, occ_ref), pf_ref[...], send_ref, own_ref, lat_ref, zf_ref)


def forward_kernel(
    feat_ref, occ_ref, grad_ref, w_ref, pf_ref, e_ref, own_ref, recv_ref, below_ref, above_ref,
    src_ref, down_ref, up_ref, send_ref, core_ref,
    out_ref, delta_ref, keep_ref, give_ref, down_own_ref, lat_ref, zf_ref,
    pool, slabs, halo, taps, terms_ref,
):
    fill_pool(own_ref, recv_ref, below_ref, above_ref, pool)
    masked = masked_of(feat_ref, occ_ref)
    build_taps(masked, pool, src_ref, down_ref, up_ref, e_ref, slabs, halo, taps)
    for b in range(NB):
        pre = jnp.dot(w_ref[...], taps[:, V * b : V * (b + 1)], preferred_element_type=F32)
        mask = occ_ref[b].astype(F32)
        sig = jax.nn.sigmoid(pre)
        out_ref[b] = (feat_ref[b].astype(F32) + mask * (pre * sig)).astype(BF16)
        delta = grad_ref[b].astype(F32) * mask * (sig * (1.0 + pre * (1.0 - sig)))
        delta_ref[b] = delta.astype(BF16)
    write_faces(delta_ref[...], pf_ref[...], send_ref, down_own_ref, lat_ref, zf_ref)
    delta = jnp.concatenate([delta_ref[b] for b in range(NB)], axis=1)
    quarter = TAPS * C // 4
    for q in range(4):
        term = lax.dot_general(
            taps[quarter * q : quarter * (q + 1), :], delta, (((1,), (1,)), ((), ())),
            preferred_element_type=F32,
        )
        if q < 3:
            terms_ref[quarter * q : quarter * (q + 1), 0:C] = term
        else:
            for i in range(3):
                terms_ref[quarter * i : quarter * (i + 1), C:128] = term[:, 32 * i : 32 * (i + 1)]
    terms_ref[3 * quarter : ROWS, :] = jnp.zeros((ROWS - 3 * quarter, 128), F32)
    core = core_ref[0]
    keep_ref[...] = terms_ref[pl.ds(pl.multiple_of(core * HALF, HALF), HALF), :]
    give_ref[...] = terms_ref[pl.ds(pl.multiple_of((1 - core) * HALF, HALF), HALF), :]


def backward_kernel(
    delta_in_ref, occ_ref, grad_ref, w_ref, e_ref, own_ref, recv_ref, below_ref, above_ref,
    src_ref, down_ref, up_ref,
    out_ref,
    pool, slabs, halo, taps,
):
    fill_pool(own_ref, recv_ref, below_ref, above_ref, pool)
    build_taps(delta_in_ref[...], pool, src_ref, down_ref, up_ref, e_ref, slabs, halo, taps)
    for b in range(NB):
        back = jnp.dot(w_ref[...], taps[:, V * b : V * (b + 1)], preferred_element_type=F32)
        out_ref[b] = (grad_ref[b].astype(F32) + occ_ref[b].astype(F32) * back).astype(BF16)


def unpack_kernel(mine_ref, other_ref, core_ref, out_ref, packed_ref):
    core = core_ref[0]
    packed_ref[pl.ds(pl.multiple_of(core * HALF, HALF), HALF), :] = mine_ref[...].astype(F32)
    packed_ref[pl.ds(pl.multiple_of((1 - core) * HALF, HALF), HALF), :] = other_ref[...].astype(F32)
    quarter = TAPS * C // 4
    for q in range(3):
        rows = slice(quarter * q, quarter * (q + 1))
        out_ref[rows, :] = packed_ref[rows, 0:C] * SCALE
        out_ref[3 * quarter :, 32 * q : 32 * (q + 1)] = packed_ref[rows, C:128] * SCALE


VM = pl.BlockSpec(memory_space=pltpu.VMEM)
SM = pl.BlockSpec(memory_space=pltpu.SMEM)


def call(kernel, ins, outs, scratch=(), flops=0, moved=0, **kw):
    return pl.pallas_call(
        kernel,
        in_specs=ins,
        out_specs=[VM] * len(outs),
        out_shape=[jax.ShapeDtypeStruct(*o) for o in outs],
        scratch_shapes=list(scratch),
        compiler_params=pltpu.CompilerParams(vmem_limit_bytes=VMEM_LIMIT),
        cost_estimate=pl.CostEstimate(flops=flops, bytes_accessed=moved, transcendentals=0),
        **kw,
    )


FACE_OUTS = [((16, C, 128), BF16), ((4, C, 128), BF16), ((2, 2, C, 128), BF16)]
SCRATCH = [
    pltpu.VMEM((35, C, 128), BF16),
    pltpu.VMEM((NB * C, 256), BF16),
    pltpu.VMEM((NB * C, V), BF16),
    pltpu.VMEM((TAPS * C, NB * V), BF16),
]


def exchange(lat, zf):
    flip2 = [(0, 1), (1, 0)]
    got = [
        lax.ppermute(lat[0], "c", flip2),
        lax.ppermute(lat[1], "zh", flip2),
        lax.ppermute(lat[2], "y", [(i, i ^ 1) for i in range(4)]),
        lax.ppermute(lat[3], "y", [(i, i ^ 2) for i in range(4)]),
    ]
    below = lax.ppermute(zf[1], BAND, [(i, i + 1) for i in range(15)])
    above = lax.ppermute(zf[0], BAND, [(i + 1, i) for i in range(15)])
    return jnp.stack(got), below, above


def exchanged(pieces, axes):
    return lax.all_to_all(pieces, axes, 0, 0, tiled=True)


def repeated(value, count):
    return jnp.broadcast_to(value[None], (count,) + value.shape)


def on_device(features, occupancy, weights, grad_out, lat_src, down_src, up_src, send_faces):
    occ = occupancy[:, None, :]
    core = lax.axis_index("c").reshape(1)
    pf = jnp.asarray(face_matrix(), BF16)
    e = jnp.asarray(halo_matrix(), BF16)
    w_fwd = weights.reshape(TAPS * C, C).T
    w_bwd = jnp.flip(weights, 0).transpose(1, 0, 2).reshape(C, TAPS * C)
    own, lat, zf = call(faces_kernel, [VM, VM, VM, SM], FACE_OUTS)(features, occ, pf, send_faces)
    recv, below, above = exchange(lat, zf)
    layer_out, delta, keep, give, down_own, lat, zf = call(
        forward_kernel,
        [VM] * 10 + [SM] * 5,
        [((NB, C, V), BF16), ((NB, C, V), BF16), ((HALF, 128), F32), ((HALF, 128), F32)] + FACE_OUTS,
        SCRATCH + [pltpu.VMEM((ROWS, 128), F32)],
    )(
        features, occ, grad_out, w_fwd, pf, e, own, recv, below, above,
        lat_src, down_src, up_src, send_faces, core,
    )
    recv, below, above = exchange(lat, zf)
    (input_grad,) = call(
        backward_kernel, [VM] * 9 + [SM] * 3, [((NB, C, V), BF16)], SCRATCH,
        flops=2 * 10**9, moved=4 * 10**6,
    )(delta, occ, grad_out, w_bwd, e, down_own, recv, below, above, lat_src, down_src, up_src)
    part = keep + lax.ppermute(give, "c", [(0, 1), (1, 0)])
    part = exchanged(part.reshape(16, HALF // 16, 128), PLANE).sum(0)
    part = exchanged(repeated(part, 8), COLUMN).sum(0)
    mine = exchanged(repeated(part.astype(BF16), 16), PLANE).reshape(HALF, 128)
    other = lax.ppermute(mine, "c", [(0, 1), (1, 0)])
    (weight_grad,) = call(
        unpack_kernel, [VM, VM, SM], [((TAPS * C, C), F32)], [pltpu.VMEM((ROWS, 128), F32)]
    )(mine, other, core)
    return layer_out, input_grad, weight_grad.reshape(TAPS, C, C)


def solution(mesh):
    fine = Mesh(mesh.devices.reshape(4, 2, 2, 4, 4), EVERY)
    split = P(EVERY)
    return jax.shard_map(
        on_device,
        mesh=fine,
        in_specs=(split, split, P(), split, split, split, split, split),
        out_specs=(split, split, P()),
        check_vma=False,
    )
```

```python
import functools
import math

import jax
import jax.numpy as jnp
import numpy as np
from jax import lax
from jax.experimental import pallas as pl
from jax.experimental.pallas import tpu as pltpu
from jax.sharding import Mesh
from jax.sharding import PartitionSpec as P

NB, C, V, TAPS = 4, 96, 512, 27
BF16, F32 = jnp.bfloat16, jnp.float32
TILE = ("y", "zh", "c")
BAND = ("zl", "x")
EVERY = TILE + BAND
PLANE = ("y", "x")
COLUMN = ("zh", "zl")
ROWS, HALF, REST = 2048, 1024, 216
MAIN = NB * V
SCALE = 1.0 / math.sqrt(1024 * 512)
SHIFTS = [(dy, dz) for dy in range(3) for dz in range(3)]
VMEM_LIMIT = 26 * 1024 * 1024


def face_matrix():
    table = np.zeros((V, 6 * 128), np.float32)
    for f in range(6):
        for a in range(8):
            for b in range(8):
                if f < 2:
                    v = 448 * f + 8 * a + b
                elif f < 4:
                    v = 64 * a + 56 * (f - 2) + b
                else:
                    v = 64 * a + 8 * b + 7 * (f - 4)
                table[v, 128 * f + 8 * a + b] = 1
                table[v, 128 * f + 64 + 8 * a + b] = 1
    return table


def lane_low(rows):
    return lax.broadcasted_iota(jnp.int32, (rows, 128), 1) < 64


def write_faces(data, pf, send_ref, own_ref, lat_refs, zf_refs, faces_z):
    flat = data.reshape(NB * C, V)
    faces = jnp.dot(flat, pf, preferred_element_type=F32).astype(BF16)
    low = lane_low(C)
    for f in range(4):
        for b in range(NB):
            own_ref[NB * f + b] = faces[C * b : C * (b + 1), 128 * f : 128 * (f + 1)]
    for d in range(2):
        for h in range(2):
            cols = slice(128 * (4 + d), 128 * (5 + d))
            first = faces[C * 2 * h : C * (2 * h + 1), cols]
            second = faces[C * (2 * h + 1) : C * (2 * h + 2), cols]
            faces_z[d, h] = jnp.where(low, first, second)
    odd = lax.axis_index("x") & 1
    zf_refs[0][...] = faces_z[1 - odd]
    zf_refs[1][...] = faces_z[odd]
    for k in range(4):
        lat_refs[k][...] = jnp.where(low, own_ref[send_ref[0, 0, k]], own_ref[send_ref[0, 1, k]])


def fill_pool(recv_refs, pool):
    low = lane_low(C)
    odd = lax.axis_index("x") & 1

    def spread(pair, at):
        turned = pltpu.roll(pair, 64, 1)
        pool[at] = jnp.where(low, pair, turned)
        pool[at + 1] = jnp.where(low, turned, pair)

    for k in range(4):
        spread(recv_refs[k][...], 16 + 2 * k)
    for h in range(2):
        spread(recv_refs[4][h], 30 - 5 * odd + 2 * h)
        spread(recv_refs[5][h], 25 + 5 * odd + 2 * h)
    for at in (24, 29, 34):
        pool[at] = jnp.zeros((C, 128), BF16)


def fill_entries(e_ref):
    lane = lax.broadcasted_iota(jnp.int32, (1, V), 1)
    row = lax.broadcasted_iota(jnp.int32, (256, V), 0)
    x, y, z = lane >> 6, (lane >> 3) & 7, lane & 7
    for t, (dy, dz) in enumerate(SHIFTS):
        if (dy, dz) == (1, 1):
            continue
        at_y, at_z = y + (dy - 1), z + (dz - 1)
        in_y, in_z = (at_y >= 0) & (at_y < 8), (at_z >= 0) & (at_z < 8)
        from_y = jnp.where(at_y < 0, 0, 64) + 8 * x + at_z
        from_z = jnp.where(at_z < 0, 128, 192) + 8 * x + at_y
        entry = jnp.where(in_z & ~in_y, from_y, jnp.where(in_y & ~in_z, from_z, -1))
        e_ref[:, V * t : V * (t + 1)] = jnp.where(row == entry, 1.0, 0.0).astype(BF16)


def build_taps(data, pool, src_ref, down_ref, up_ref, e_ref, slabs, halo, taps):
    low = lane_low(C)
    side_x = []
    for b in range(NB):
        lat = [pool[jnp.where(src_ref[b, i] < 0, 24, src_ref[b, i])] for i in range(4)]
        below = pool[jnp.where(down_ref[b] < 0, 29, 25 + down_ref[b])]
        above = pool[jnp.where(up_ref[b] < 0, 34, 30 + up_ref[b])]
        side_x.append(jnp.where(low, lat[0], lat[1]))
        slabs[C * b : C * (b + 1), 0:128] = jnp.where(low, lat[2], lat[3])
        slabs[C * b : C * (b + 1), 128:256] = jnp.where(low, below, above)
    lanes = lax.broadcasted_iota(jnp.int32, (C, V), 1)
    lane_y, lane_z = (lanes >> 3) & 7, lanes & 7
    for t, (dy, dz) in enumerate(SHIFTS):
        rows = slice(C * t, C * (t + 1))
        step = 8 * (dy - 1) + dz - 1
        if step:
            halo[...] = jnp.dot(
                slabs[...], e_ref[:, V * t : V * (t + 1)], preferred_element_type=F32
            ).astype(BF16)
            at_y, at_z = lane_y + (dy - 1), lane_z + (dz - 1)
            inside = (at_y >= 0) & (at_y < 8) & (at_z >= 0) & (at_z < 8)
        for b in range(NB):
            if step:
                shifted = pltpu.roll(data[b], (-step) % V, 1)
                shifted = jnp.where(inside, shifted, halo[C * b : C * (b + 1), :])
                edge = pltpu.roll(side_x[b], (-step) % 128, 1)
                edge = jnp.where(inside[:, :128], edge, jnp.zeros_like(edge))
            else:
                shifted, edge = data[b], side_x[b]
            taps[rows, V * b : V * (b + 1)] = shifted
            taps[rows, MAIN + 128 * b : MAIN + 128 * (b + 1)] = edge


def convolve(w3, taps, ends, finish):
    low = lane_low(C)
    ends[...] = jnp.dot(w3[: 2 * C, :], taps[:, MAIN:], preferred_element_type=F32)
    for b in range(NB):
        y = jnp.dot(w3[...], taps[:, V * b : V * (b + 1)], preferred_element_type=F32)
        place = slice(128 * b, 128 * (b + 1))
        tiles = [slice(128 * i, 128 * (i + 1)) for i in range(4)]
        before = [ends[:C, place]] + [pltpu.roll(y[:C, tile], 64, 1) for tile in tiles]
        after = [pltpu.roll(y[C : 2 * C, tile], 64, 1) for tile in tiles] + [ends[C:, place]]
        parts = [
            y[2 * C :, tiles[i]]
            + jnp.where(low, before[i], before[i + 1])
            + jnp.where(low, after[i], after[i + 1])
            for i in range(4)
        ]
        finish(b, jnp.concatenate(parts, axis=1))


def kernel_terms(taps, delta_ref, around, terms_ref):
    low = lane_low(C)
    zero = jnp.zeros((C, 128), BF16)
    for b in range(NB):
        tiles = [delta_ref[b, :, 128 * i : 128 * (i + 1)] for i in range(4)]
        turned = [pltpu.roll(tile, 64, 1) for tile in tiles]
        for i in range(4):
            place = slice(V * b + 128 * i, V * b + 128 * (i + 1))
            around[:C, place] = jnp.where(low, turned[i], turned[i + 1] if i < 3 else zero)
            around[C:, place] = jnp.where(low, turned[i - 1] if i else zero, turned[i])
        place = slice(MAIN + 128 * b, MAIN + 128 * (b + 1))
        around[:C, place] = jnp.where(low, tiles[0], zero)
        around[C:, place] = jnp.where(low, zero, tiles[3])
    over_lanes = (((1,), (1,)), ((), ()))
    rows = 9 * C
    sides = lax.dot_general(taps[...], around[...], over_lanes, preferred_element_type=F32)
    terms_ref[0:rows, :] = sides[:, 0:128]
    terms_ref[rows : 2 * rows, 0:64] = sides[:, 128:192]
    delta = jnp.concatenate([delta_ref[b] for b in range(NB)], axis=1)
    middle = lax.dot_general(taps[:, :MAIN], delta, over_lanes, preferred_element_type=F32)
    terms_ref[rows : 2 * rows, 64:128] = middle[:, 0:64]
    for g in range(4):
        terms_ref[2 * rows : 2 * rows + REST, 32 * g : 32 * (g + 1)] = middle[
            REST * g : REST * (g + 1), 64:C
        ]
    terms_ref[2 * rows + REST :, :] = jnp.zeros((ROWS - 2 * rows - REST, 128), F32)


def masked_of(feat_ref, occ_ref):
    occ = occ_ref[...].astype(F32).astype(BF16)
    return jnp.stack([feat_ref[b] * occ[b : b + 1, :] for b in range(NB)])


def started(sems, *pairs):
    copies = [pltpu.make_async_copy(a, b, sems.at[i]) for i, (a, b) in enumerate(pairs)]
    for copy in copies:
        copy.start()
    return copies


def waited(*copies):
    for copy in copies:
        copy.wait()


def faces_kernel(feat_in, occ_in, pf_in, send_in, own_ref, *refs):
    feat, occ, pf, send, faces_z, sems = refs[6:]
    waited(*started(sems, (send_in, send), (occ_in, occ), (feat_in, feat), (pf_in, pf)))
    write_faces(masked_of(feat, occ), pf[...], send, own_ref, refs[:4], refs[4:6], faces_z)


def forward_kernel(
    feat_in, occ_in, grad_in, w_in, pf_in, src_in, down_in, up_in, send_in,
    own_ref, recv0, recv1, recv2, recv3, recv4, recv5,
    out_out, delta_ref, keep_ref, give_ref, delta_own_ref, lat0, lat1, lat2, lat3, zf0, zf1,
    occ, grad, w, src, down, up, out, pool, slabs, halo, taps, w3, e, ends, sems, out_sems,
    feat, pf, send, faces_z, terms_ref, around,
):
    early = started(
        sems, (src_in, src), (down_in, down), (up_in, up), (occ_in, occ), (feat_in, feat),
    )
    later = started(sems.at[5:], (w_in, w), (grad_in, grad), (pf_in, pf), (send_in, send))
    for i in range(16):
        pool[i] = own_ref[i]
    fill_pool((recv0, recv1, recv2, recv3, recv4, recv5), pool)
    fill_entries(e)
    waited(*early)
    build_taps(masked_of(feat, occ), pool, src, down, up, e, slabs, halo, taps)
    waited(*later)
    for i, dx in enumerate((0, 2, 1)):
        w3[C * i : C * (i + 1), :] = w[9 * dx : 9 * (dx + 1)].reshape(9 * C, C).T
    leaving = []

    def finish(b, pre):
        mask = occ[b : b + 1, :].astype(F32)
        sig = jax.nn.sigmoid(pre)
        out[b] = (feat[b].astype(F32) + mask * (pre * sig)).astype(BF16)
        leaving.extend(started(out_sems.at[b:], (out.at[b], out_out.at[b])))
        delta = grad[b].astype(F32) * mask * (sig * (1.0 + pre * (1.0 - sig)))
        delta_ref[b] = delta.astype(BF16)

    convolve(w3, taps, ends, finish)
    write_faces(
        delta_ref[...], pf[...], send, delta_own_ref, (lat0, lat1, lat2, lat3), (zf0, zf1), faces_z
    )
    kernel_terms(taps, delta_ref, around, terms_ref)
    core = lax.axis_index("c")
    keep_ref[...] = terms_ref[pl.ds(pl.multiple_of(core * HALF, HALF), HALF), :]
    give_ref[...] = terms_ref[pl.ds(pl.multiple_of((1 - core) * HALF, HALF), HALF), :]
    waited(*leaving)


def backward_kernel(
    occ_in, grad_in, w_in, src_in, down_in, up_in, delta_in, own_in,
    recv0, recv1, recv2, recv3, recv4, recv5,
    out_out,
    occ, grad, w, src, down, up, out, pool, slabs, halo, taps, w3, e, ends, sems, out_sems,
    delta, lateral, vertical,
):
    early = started(
        sems,
        *[(recv, lateral.at[k]) for k, recv in enumerate((recv0, recv1, recv2, recv3))],
        (recv4, vertical.at[0]), (recv5, vertical.at[1]), (own_in, pool.at[0:16]),
        (src_in, src), (down_in, down), (up_in, up), (delta_in, delta),
    )
    later = started(sems.at[11:], (w_in, w), (grad_in, grad), (occ_in, occ))
    fill_entries(e)
    waited(*early)
    fill_pool([lateral.at[k] for k in range(4)] + [vertical.at[0], vertical.at[1]], pool)
    build_taps(delta[...], pool, src, down, up, e, slabs, halo, taps)
    waited(*later)
    for i, dx in enumerate((0, 2, 1)):
        last = TAPS - 1 - 9 * dx
        w3[C * i : C * (i + 1), :] = jnp.concatenate([w[last - t] for t in range(9)], axis=1)
    leaving = []

    def finish(b, back):
        mask = occ[b : b + 1, :].astype(F32)
        out[b] = (grad[b].astype(F32) + mask * back).astype(BF16)
        leaving.extend(started(out_sems.at[b:], (out.at[b], out_out.at[b])))

    convolve(w3, taps, ends, finish)
    waited(*leaving)


def sum_kernel(pieces_ref, out_ref):
    total = pieces_ref[0]
    for i in range(1, pieces_ref.shape[0]):
        total = total + pieces_ref[i]
    total = total.astype(out_ref.dtype)
    for i in range(out_ref.shape[0]):
        out_ref[i] = total


def unpack_kernel(mine_ref, other_ref, out_ref, packed):
    core = lax.axis_index("c")
    packed[pl.ds(pl.multiple_of(core * HALF, HALF), HALF), :] = mine_ref[...].astype(F32) * SCALE
    packed[pl.ds(pl.multiple_of((1 - core) * HALF, HALF), HALF), :] = other_ref[...].astype(F32) * SCALE
    rows = 9 * C
    out_ref[0:rows, :] = packed[0:rows, 0:C]
    out_ref[2 * rows :, 0:32] = packed[0:rows, C:128]
    out_ref[2 * rows :, 32:C] = packed[rows : 2 * rows, 0:64]
    out_ref[rows : 2 * rows, 0:64] = packed[rows : 2 * rows, 64:128]
    for g in range(4):
        out_ref[rows + REST * g : rows + REST * (g + 1), 64:C] = packed[
            2 * rows : 2 * rows + REST, 32 * g : 32 * (g + 1)
        ]


VM = pl.BlockSpec(memory_space=pltpu.VMEM)
HB = pl.BlockSpec(memory_space=pltpu.HBM)
MIB = 1024 * 1024


def call(kernel, ins, outs, scratch=(), flops=0, moved=0, limit=8 * MIB):
    return pl.pallas_call(
        kernel,
        in_specs=ins,
        out_specs=[spec for spec, _, _ in outs],
        out_shape=[jax.ShapeDtypeStruct(shape, kind) for _, shape, kind in outs],
        scratch_shapes=list(scratch),
        compiler_params=pltpu.CompilerParams(vmem_limit_bytes=limit),
        cost_estimate=pl.CostEstimate(flops=flops, bytes_accessed=moved, transcendentals=0),
    )


FACE_OUTS = [(VM, (16, C, 128), BF16)] + [(VM, (C, 128), BF16)] * 4 + [(VM, (2, C, 128), BF16)] * 2
BLOCKS = (NB, C, V)
FEAT, OCC = pltpu.VMEM(BLOCKS, BF16), pltpu.VMEM((NB, V), jnp.int32)
PF, SEND = pltpu.VMEM((V, 768), BF16), pltpu.SMEM((1, 2, 4), jnp.int32)
FACES_Z = pltpu.VMEM((2, 2, C, 128), BF16)
SCRATCH = [
    OCC,
    pltpu.VMEM(BLOCKS, BF16),
    pltpu.VMEM((TAPS, C, C), BF16),
    pltpu.SMEM((NB, 4), jnp.int32),
    pltpu.SMEM((NB,), jnp.int32),
    pltpu.SMEM((NB,), jnp.int32),
    pltpu.VMEM(BLOCKS, BF16),
    pltpu.VMEM((35, C, 128), BF16),
    pltpu.VMEM((NB * C, 256), BF16),
    pltpu.VMEM((NB * C, V), BF16),
    pltpu.VMEM((9 * C, MAIN + NB * 128), BF16),
    pltpu.VMEM((3 * C, 9 * C), BF16),
    pltpu.VMEM((256, 9 * V), BF16),
    pltpu.VMEM((2 * C, NB * 128), F32),
    pltpu.SemaphoreType.DMA((16,)),
    pltpu.SemaphoreType.DMA((NB,)),
]


def exchange(lat0, lat1, lat2, lat3, zf0, zf1):
    pairs = [(i, i + 1) for i in range(16)]
    flip2 = [(0, 1), (1, 0)]
    return [
        lax.ppermute(lat0, "c", flip2),
        lax.ppermute(lat1, "zh", flip2),
        lax.ppermute(lat2, "y", [(i, i ^ 1) for i in range(4)]),
        lax.ppermute(lat3, "y", [(i, i ^ 2) for i in range(4)]),
        lax.ppermute(zf0, BAND, [p for i, j in pairs[0:15:2] for p in ((i, j), (j, i))]),
        lax.ppermute(zf1, BAND, [p for i, j in pairs[1:15:2] for p in ((i, j), (j, i))]),
    ]


def exchanged(pieces, axes):
    return lax.all_to_all(pieces, axes, 0, 0, tiled=True)


def summed(pieces, count, kind):
    (out,) = call(
        sum_kernel, [VM], [(VM, (count, 64, 128), kind)], flops=pieces.size, moved=4 * pieces.size
    )(pieces)
    return out


def in_hbm(*values):
    return [pltpu.with_memory_space_constraint(value, pltpu.HBM) for value in values]


def on_device(features, occupancy, weights, grad_out, lat_src, down_src, up_src, send_faces):
    pf = jnp.asarray(face_matrix(), BF16)
    sends = send_faces.transpose(0, 2, 1)
    own, *out = call(
        faces_kernel, [HB] * 4, FACE_OUTS,
        [FEAT, OCC, PF, SEND, FACES_Z, pltpu.SemaphoreType.DMA((4,))],
    )(*in_hbm(features, occupancy, pf, sends))
    half = (VM, (HALF, 128), F32)
    layer_out, delta, keep, give, delta_own, *out = call(
        forward_kernel,
        [HB] * 9 + [VM] * 7,
        [(HB, BLOCKS, BF16), (VM, BLOCKS, BF16), half, half] + FACE_OUTS,
        SCRATCH
        + [FEAT, PF, SEND, FACES_Z, pltpu.VMEM((ROWS, 128), F32)]
        + [pltpu.VMEM((2 * C, MAIN + NB * 128), BF16)],
        limit=VMEM_LIMIT,
    )(
        *in_hbm(features, occupancy, grad_out, weights, pf, lat_src, down_src, up_src, sends),
        own,
        *exchange(*out),
    )
    halos = exchange(*out)
    part = keep + lax.ppermute(give, "c", [(0, 1), (1, 0)])
    part = exchanged(part.reshape(16, HALF // 16, 128), PLANE)
    part, *halos[:4] = lax.optimization_barrier((part, *halos[:4]))
    part = exchanged(summed(part, 8, F32), COLUMN)
    part, *halos[4:] = lax.optimization_barrier((part, *halos[4:]))
    part = exchanged(summed(part, 16, BF16), PLANE)
    (input_grad,) = call(
        backward_kernel,
        [HB] * 14,
        [(HB, BLOCKS, BF16)],
        SCRATCH + [FEAT, pltpu.VMEM((4, C, 128), BF16), pltpu.VMEM((2, 2, C, 128), BF16)],
        flops=5 * 10**9, moved=4 * 10**6, limit=VMEM_LIMIT,
    )(
        *in_hbm(occupancy, grad_out, weights, lat_src, down_src, up_src, delta, delta_own),
        *in_hbm(*halos),
    )
    mine, input_grad = lax.optimization_barrier((part.reshape(HALF, 128), input_grad))
    other = lax.ppermute(mine, "c", [(0, 1), (1, 0)])
    (weight_grad,) = call(
        unpack_kernel, [VM, VM], [(VM, (TAPS * C, C), F32)], [pltpu.VMEM((ROWS, 128), F32)]
    )(mine, other)
    return layer_out, input_grad, weight_grad.reshape(TAPS, C, C)


def solution(mesh):
    fine = Mesh(mesh.devices.reshape(4, 2, 2, 4, 4), EVERY)
    split = P(EVERY)
    return jax.shard_map(
        on_device,
        mesh=fine,
        in_specs=(split, split, P(), split, split, split, split, split),
        out_specs=(split, split, P()),
        check_vma=False,
    )
```

```python
import functools
import math

import jax
import jax.numpy as jnp
import numpy as np
from jax import lax
from jax.experimental import pallas as pl
from jax.experimental.pallas import tpu as pltpu
from jax.sharding import Mesh
from jax.sharding import PartitionSpec as P

NB, C, V, TAPS = 4, 96, 512, 27
BF16, F32 = jnp.bfloat16, jnp.float32
TILE = ("y", "zh", "c")
BAND = ("zl", "x")
EVERY = TILE + BAND
PLANE = ("y", "x")
COLUMN = ("zh", "zl")
ROWS, HALF, REST = 2048, 1024, 216
MAIN = NB * V
SCALE = 1.0 / math.sqrt(1024 * 512)
SHIFTS = [(dy, dz) for dy in range(3) for dz in range(3)]
VMEM_LIMIT = 26 * 1024 * 1024


def face_matrix():
    table = np.zeros((V, 6 * 128), np.float32)
    for f in range(6):
        for a in range(8):
            for b in range(8):
                if f < 2:
                    v = 448 * f + 8 * a + b
                elif f < 4:
                    v = 64 * a + 56 * (f - 2) + b
                else:
                    v = 64 * a + 8 * b + 7 * (f - 4)
                table[v, 128 * f + 8 * a + b] = 1
                table[v, 128 * f + 64 + 8 * a + b] = 1
    return table


def lane_low(rows):
    return lax.broadcasted_iota(jnp.int32, (rows, 128), 1) < 64


def write_faces(data, pf, send_ref, own_ref, lat_refs, zf_refs, faces_z):
    flat = data.reshape(NB * C, V)
    faces = jnp.dot(flat, pf, preferred_element_type=F32).astype(BF16)
    low = lane_low(C)
    for f in range(4):
        for b in range(NB):
            own_ref[NB * f + b] = faces[C * b : C * (b + 1), 128 * f : 128 * (f + 1)]
    for d in range(2):
        for h in range(2):
            cols = slice(128 * (4 + d), 128 * (5 + d))
            first = faces[C * 2 * h : C * (2 * h + 1), cols]
            second = faces[C * (2 * h + 1) : C * (2 * h + 2), cols]
            faces_z[d, h] = jnp.where(low, first, second)
    odd = lax.axis_index("x") & 1
    zf_refs[0][...] = faces_z[1 - odd]
    zf_refs[1][...] = faces_z[odd]
    for k in range(4):
        lat_refs[k][...] = jnp.where(low, own_ref[send_ref[0, 0, k]], own_ref[send_ref[0, 1, k]])


def fill_pool(recv_refs, pool):
    low = lane_low(C)
    odd = lax.axis_index("x") & 1

    def spread(pair, at):
        turned = pltpu.roll(pair, 64, 1)
        pool[at] = jnp.where(low, pair, turned)
        pool[at + 1] = jnp.where(low, turned, pair)

    for k in range(4):
        spread(recv_refs[k][...], 16 + 2 * k)
    for h in range(2):
        spread(recv_refs[4][h], 30 - 5 * odd + 2 * h)
        spread(recv_refs[5][h], 25 + 5 * odd + 2 * h)
    for at in (24, 29, 34):
        pool[at] = jnp.zeros((C, 128), BF16)


def fill_entries(e_ref):
    lane = lax.broadcasted_iota(jnp.int32, (1, V), 1)
    row = lax.broadcasted_iota(jnp.int32, (256, V), 0)
    x, y, z = lane >> 6, (lane >> 3) & 7, lane & 7
    for t, (dy, dz) in enumerate(SHIFTS):
        if (dy, dz) == (1, 1):
            continue
        at_y, at_z = y + (dy - 1), z + (dz - 1)
        in_y, in_z = (at_y >= 0) & (at_y < 8), (at_z >= 0) & (at_z < 8)
        from_y = jnp.where(at_y < 0, 0, 64) + 8 * x + at_z
        from_z = jnp.where(at_z < 0, 128, 192) + 8 * x + at_y
        entry = jnp.where(in_z & ~in_y, from_y, jnp.where(in_y & ~in_z, from_z, -1))
        e_ref[:, V * t : V * (t + 1)] = jnp.where(row == entry, 1.0, 0.0).astype(BF16)


def build_taps(data, pool, src_ref, down_ref, up_ref, e_ref, slabs, halo, taps):
    low = lane_low(C)
    side_x = []
    for b in range(NB):
        lat = [pool[jnp.where(src_ref[b, i] < 0, 24, src_ref[b, i])] for i in range(4)]
        below = pool[jnp.where(down_ref[b] < 0, 29, 25 + down_ref[b])]
        above = pool[jnp.where(up_ref[b] < 0, 34, 30 + up_ref[b])]
        side_x.append(jnp.where(low, lat[0], lat[1]))
        slabs[C * b : C * (b + 1), 0:128] = jnp.where(low, lat[2], lat[3])
        slabs[C * b : C * (b + 1), 128:256] = jnp.where(low, below, above)
    lanes = lax.broadcasted_iota(jnp.int32, (C, V), 1)
    lane_y, lane_z = (lanes >> 3) & 7, lanes & 7
    for t, (dy, dz) in enumerate(SHIFTS):
        rows = slice(C * t, C * (t + 1))
        step = 8 * (dy - 1) + dz - 1
        if step:
            halo[...] = jnp.dot(
                slabs[...], e_ref[:, V * t : V * (t + 1)], preferred_element_type=F32
            ).astype(BF16)
            at_y, at_z = lane_y + (dy - 1), lane_z + (dz - 1)
            inside = (at_y >= 0) & (at_y < 8) & (at_z >= 0) & (at_z < 8)
        for b in range(NB):
            if step:
                shifted = pltpu.roll(data[b], (-step) % V, 1)
                shifted = jnp.where(inside, shifted, halo[C * b : C * (b + 1), :])
                edge = pltpu.roll(side_x[b], (-step) % 128, 1)
                edge = jnp.where(inside[:, :128], edge, jnp.zeros_like(edge))
            else:
                shifted, edge = data[b], side_x[b]
            taps[rows, V * b : V * (b + 1)] = shifted
            taps[rows, MAIN + 128 * b : MAIN + 128 * (b + 1)] = edge


def convolve(w3, taps, ends, finish):
    low = lane_low(C)
    ends[...] = jnp.dot(w3[: 2 * C, :], taps[:, MAIN:], preferred_element_type=F32)
    for b in range(NB):
        y = jnp.dot(w3[...], taps[:, V * b : V * (b + 1)], preferred_element_type=F32)
        place = slice(128 * b, 128 * (b + 1))
        tiles = [slice(128 * i, 128 * (i + 1)) for i in range(4)]
        before = [ends[:C, place]] + [pltpu.roll(y[:C, tile], 64, 1) for tile in tiles]
        after = [pltpu.roll(y[C : 2 * C, tile], 64, 1) for tile in tiles] + [ends[C:, place]]
        parts = [
            y[2 * C :, tiles[i]]
            + jnp.where(low, before[i], before[i + 1])
            + jnp.where(low, after[i], after[i + 1])
            for i in range(4)
        ]
        finish(b, jnp.concatenate(parts, axis=1))


def kernel_terms(taps, delta_ref, around, terms_ref):
    low = lane_low(C)
    zero = jnp.zeros((C, 128), BF16)
    for b in range(NB):
        tiles = [delta_ref[b, :, 128 * i : 128 * (i + 1)] for i in range(4)]
        turned = [pltpu.roll(tile, 64, 1) for tile in tiles]
        for i in range(4):
            place = slice(V * b + 128 * i, V * b + 128 * (i + 1))
            around[:C, place] = jnp.where(low, turned[i], turned[i + 1] if i < 3 else zero)
            around[C:, place] = jnp.where(low, turned[i - 1] if i else zero, turned[i])
        place = slice(MAIN + 128 * b, MAIN + 128 * (b + 1))
        around[:C, place] = jnp.where(low, tiles[0], zero)
        around[C:, place] = jnp.where(low, zero, tiles[3])
    over_lanes = (((1,), (1,)), ((), ()))
    rows = 9 * C
    sides = lax.dot_general(taps[...], around[...], over_lanes, preferred_element_type=F32)
    terms_ref[0:rows, :] = sides[:, 0:128]
    terms_ref[rows : 2 * rows, 0:64] = sides[:, 128:192]
    delta = jnp.concatenate([delta_ref[b] for b in range(NB)], axis=1)
    middle = lax.dot_general(taps[:, :MAIN], delta, over_lanes, preferred_element_type=F32)
    terms_ref[rows : 2 * rows, 64:128] = middle[:, 0:64]
    for g in range(4):
        terms_ref[2 * rows : 2 * rows + REST, 32 * g : 32 * (g + 1)] = middle[
            REST * g : REST * (g + 1), 64:C
        ]
    terms_ref[2 * rows + REST :, :] = jnp.zeros((ROWS - 2 * rows - REST, 128), F32)


def masked_of(feat_ref, occ_ref):
    occ = occ_ref[...].astype(F32).astype(BF16)
    return jnp.stack([feat_ref[b] * occ[b : b + 1, :] for b in range(NB)])


def started(sems, *pairs):
    copies = [pltpu.make_async_copy(a, b, sems.at[i]) for i, (a, b) in enumerate(pairs)]
    for copy in copies:
        copy.start()
    return copies


def waited(*copies):
    for copy in copies:
        copy.wait()


def faces_kernel(feat_in, occ_in, pf_in, send_in, masked_ref, own_ref, *refs):
    feat, occ, pf, send, faces_z, sems = refs[6:]
    copies = started(sems, (send_in, send), (occ_in, occ), (feat_in, feat), (pf_in, pf))
    waited(*copies[1:3])
    masked_ref[...] = masked_of(feat, occ)
    waited(copies[0], copies[3])
    write_faces(masked_ref[...], pf[...], send, own_ref, refs[:4], refs[4:6], faces_z)


def forward_kernel(
    feat_in, occ_in, grad_in, w_in, pf_in, src_in, down_in, up_in, send_in,
    masked_ref, own_ref, recv0, recv1, recv2, recv3, recv4, recv5,
    out_out, delta_ref, keep_ref, give_ref, delta_own_ref, lat0, lat1, lat2, lat3, zf0, zf1,
    occ, grad, w, src, down, up, out, pool, slabs, halo, taps, w3, e, ends, sems, out_sems,
    feat, pf, send, faces_z, terms_ref, around,
):
    early = started(sems, (src_in, src), (down_in, down), (up_in, up))
    later = started(
        sems.at[3:], (w_in, w), (occ_in, occ), (feat_in, feat), (grad_in, grad), (pf_in, pf), (send_in, send)
    )
    for i in range(16):
        pool[i] = own_ref[i]
    fill_pool((recv0, recv1, recv2, recv3, recv4, recv5), pool)
    fill_entries(e)
    waited(*early)
    build_taps(masked_ref[...], pool, src, down, up, e, slabs, halo, taps)
    waited(*later)
    for i, dx in enumerate((0, 2, 1)):
        w3[C * i : C * (i + 1), :] = w[9 * dx : 9 * (dx + 1)].reshape(9 * C, C).T
    leaving = []

    def finish(b, pre):
        mask = occ[b : b + 1, :].astype(F32)
        sig = jax.nn.sigmoid(pre)
        out[b] = (feat[b].astype(F32) + mask * (pre * sig)).astype(BF16)
        leaving.extend(started(out_sems.at[b:], (out.at[b], out_out.at[b])))
        delta = grad[b].astype(F32) * mask * (sig * (1.0 + pre * (1.0 - sig)))
        delta_ref[b] = delta.astype(BF16)

    convolve(w3, taps, ends, finish)
    write_faces(
        delta_ref[...], pf[...], send, delta_own_ref, (lat0, lat1, lat2, lat3), (zf0, zf1), faces_z
    )
    kernel_terms(taps, delta_ref, around, terms_ref)
    core = lax.axis_index("c")
    keep_ref[...] = terms_ref[pl.ds(pl.multiple_of(core * HALF, HALF), HALF), :]
    give_ref[...] = terms_ref[pl.ds(pl.multiple_of((1 - core) * HALF, HALF), HALF), :]
    waited(*leaving)


def backward_kernel(
    occ_in, grad_in, w_in, src_in, down_in, up_in, delta_in, own_in,
    recv0, recv1, recv2, recv3, recv4, recv5,
    out_out,
    occ, grad, w, src, down, up, out, pool, slabs, halo, taps, w3, e, ends, sems, out_sems,
    delta, lateral, vertical,
):
    early = started(
        sems,
        *[(recv, lateral.at[k]) for k, recv in enumerate((recv0, recv1, recv2, recv3))],
        (recv4, vertical.at[0]), (recv5, vertical.at[1]), (own_in, pool.at[0:16]),
        (src_in, src), (down_in, down), (up_in, up), (delta_in, delta),
    )
    later = started(sems.at[11:], (w_in, w), (grad_in, grad), (occ_in, occ))
    fill_entries(e)
    waited(*early)
    fill_pool([lateral.at[k] for k in range(4)] + [vertical.at[0], vertical.at[1]], pool)
    build_taps(delta[...], pool, src, down, up, e, slabs, halo, taps)
    waited(*later)
    for i, dx in enumerate((0, 2, 1)):
        last = TAPS - 1 - 9 * dx
        w3[C * i : C * (i + 1), :] = jnp.concatenate([w[last - t] for t in range(9)], axis=1)
    leaving = []

    def finish(b, back):
        mask = occ[b : b + 1, :].astype(F32)
        out[b] = (grad[b].astype(F32) + mask * back).astype(BF16)
        leaving.extend(started(out_sems.at[b:], (out.at[b], out_out.at[b])))

    convolve(w3, taps, ends, finish)
    waited(*leaving)


def sum_kernel(pieces_ref, out_ref):
    total = pieces_ref[0]
    for i in range(1, pieces_ref.shape[0]):
        total = total + pieces_ref[i]
    total = total.astype(out_ref.dtype)
    for i in range(out_ref.shape[0]):
        out_ref[i] = total


def unpack_kernel(mine_ref, other_ref, out_out, packed, out, sems):
    core = lax.axis_index("c")
    packed[pl.ds(pl.multiple_of(core * HALF, HALF), HALF), :] = mine_ref[...].astype(F32) * SCALE
    packed[pl.ds(pl.multiple_of((1 - core) * HALF, HALF), HALF), :] = other_ref[...].astype(F32) * SCALE
    rows = 9 * C
    third = [pl.ds(rows * i, rows) for i in range(3)]
    out[0:rows, :] = packed[0:rows, 0:C]
    leaving = started(sems, (out.at[third[0]], out_out.at[third[0]]))
    out[2 * rows :, 0:32] = packed[0:rows, C:128]
    out[2 * rows :, 32:C] = packed[rows : 2 * rows, 0:64]
    leaving += started(sems.at[1:], (out.at[third[2]], out_out.at[third[2]]))
    out[rows : 2 * rows, 0:64] = packed[rows : 2 * rows, 64:128]
    for g in range(4):
        out[rows + REST * g : rows + REST * (g + 1), 64:C] = packed[
            2 * rows : 2 * rows + REST, 32 * g : 32 * (g + 1)
        ]
    leaving += started(sems.at[2:], (out.at[third[1]], out_out.at[third[1]]))
    waited(*leaving)


VM = pl.BlockSpec(memory_space=pltpu.VMEM)
HB = pl.BlockSpec(memory_space=pltpu.HBM)
MIB = 1024 * 1024


def call(kernel, ins, outs, scratch=(), flops=0, moved=0, limit=8 * MIB):
    return pl.pallas_call(
        kernel,
        in_specs=ins,
        out_specs=[spec for spec, _, _ in outs],
        out_shape=[jax.ShapeDtypeStruct(shape, kind) for _, shape, kind in outs],
        scratch_shapes=list(scratch),
        compiler_params=pltpu.CompilerParams(vmem_limit_bytes=limit),
        cost_estimate=pl.CostEstimate(flops=flops, bytes_accessed=moved, transcendentals=0),
    )


FACE_OUTS = [(VM, (16, C, 128), BF16)] + [(VM, (C, 128), BF16)] * 4 + [(VM, (2, C, 128), BF16)] * 2
BLOCKS = (NB, C, V)
FEAT, OCC = pltpu.VMEM(BLOCKS, BF16), pltpu.VMEM((NB, V), jnp.int32)
PF, SEND = pltpu.VMEM((V, 768), BF16), pltpu.SMEM((1, 2, 4), jnp.int32)
FACES_Z = pltpu.VMEM((2, 2, C, 128), BF16)
SCRATCH = [
    OCC,
    pltpu.VMEM(BLOCKS, BF16),
    pltpu.VMEM((TAPS, C, C), BF16),
    pltpu.SMEM((NB, 4), jnp.int32),
    pltpu.SMEM((NB,), jnp.int32),
    pltpu.SMEM((NB,), jnp.int32),
    pltpu.VMEM(BLOCKS, BF16),
    pltpu.VMEM((35, C, 128), BF16),
    pltpu.VMEM((NB * C, 256), BF16),
    pltpu.VMEM((NB * C, V), BF16),
    pltpu.VMEM((9 * C, MAIN + NB * 128), BF16),
    pltpu.VMEM((3 * C, 9 * C), BF16),
    pltpu.VMEM((256, 9 * V), BF16),
    pltpu.VMEM((2 * C, NB * 128), F32),
    pltpu.SemaphoreType.DMA((16,)),
    pltpu.SemaphoreType.DMA((NB,)),
]


def exchange(lat0, lat1, lat2, lat3, zf0, zf1):
    pairs = [(i, i + 1) for i in range(16)]
    flip2 = [(0, 1), (1, 0)]
    return [
        lax.ppermute(lat0, "c", flip2),
        lax.ppermute(lat1, "zh", flip2),
        lax.ppermute(lat2, "y", [(i, i ^ 1) for i in range(4)]),
        lax.ppermute(lat3, "y", [(i, i ^ 2) for i in range(4)]),
        lax.ppermute(zf0, BAND, [p for i, j in pairs[0:15:2] for p in ((i, j), (j, i))]),
        lax.ppermute(zf1, BAND, [p for i, j in pairs[1:15:2] for p in ((i, j), (j, i))]),
    ]


def exchanged(pieces, axes):
    return lax.all_to_all(pieces, axes, 0, 0, tiled=True)


def summed(pieces, count, kind):
    (out,) = call(
        sum_kernel, [VM], [(VM, (count, 64, 128), kind)], flops=pieces.size, moved=4 * pieces.size
    )(pieces)
    return out


def in_hbm(*values):
    return [pltpu.with_memory_space_constraint(value, pltpu.HBM) for value in values]


def on_device(features, occupancy, weights, grad_out, lat_src, down_src, up_src, send_faces):
    pf = jnp.asarray(face_matrix(), BF16)
    sends = send_faces.transpose(0, 2, 1)
    masked, own, *out = call(
        faces_kernel, [HB] * 4, [(VM, BLOCKS, BF16)] + FACE_OUTS,
        [FEAT, OCC, PF, SEND, FACES_Z, pltpu.SemaphoreType.DMA((4,))],
    )(*in_hbm(features, occupancy, pf, sends))
    half = (VM, (HALF, 128), F32)
    layer_out, delta, keep, give, delta_own, *out = call(
        forward_kernel,
        [HB] * 9 + [VM] * 8,
        [(HB, BLOCKS, BF16), (VM, BLOCKS, BF16), half, half] + FACE_OUTS,
        SCRATCH
        + [FEAT, PF, SEND, FACES_Z, pltpu.VMEM((ROWS, 128), F32)]
        + [pltpu.VMEM((2 * C, MAIN + NB * 128), BF16)],
        limit=VMEM_LIMIT,
    )(
        *in_hbm(features, occupancy, grad_out, weights, pf, lat_src, down_src, up_src, sends),
        masked,
        own,
        *exchange(*out),
    )
    halos = exchange(*out)
    part = keep + lax.ppermute(give, "c", [(0, 1), (1, 0)])
    part = exchanged(part.reshape(16, HALF // 16, 128), PLANE)
    part, halos[1], halos[2], halos[4] = lax.optimization_barrier((part, halos[1], halos[2], halos[4]))
    part = exchanged(summed(part, 8, F32), COLUMN)
    part, halos[0], halos[3], halos[5] = lax.optimization_barrier((part, halos[0], halos[3], halos[5]))
    part = exchanged(summed(part, 16, BF16), PLANE)
    (input_grad,) = call(
        backward_kernel,
        [HB] * 14,
        [(HB, BLOCKS, BF16)],
        SCRATCH + [FEAT, pltpu.VMEM((4, C, 128), BF16), pltpu.VMEM((2, 2, C, 128), BF16)],
        flops=5 * 10**9, moved=4 * 10**6, limit=VMEM_LIMIT,
    )(
        *in_hbm(occupancy, grad_out, weights, lat_src, down_src, up_src, delta, delta_own),
        *in_hbm(*halos),
    )
    mine, input_grad = lax.optimization_barrier((part.reshape(HALF, 128), input_grad))
    other = lax.ppermute(mine, "c", [(0, 1), (1, 0)])
    (weight_grad,) = call(
        unpack_kernel, [VM, VM], [(HB, (TAPS * C, C), F32)],
        [pltpu.VMEM((ROWS, 128), F32), pltpu.VMEM((TAPS * C, C), F32), pltpu.SemaphoreType.DMA((3,))],
    )(mine, other)
    return layer_out, input_grad, weight_grad.reshape(TAPS, C, C)


def solution(mesh):
    fine = Mesh(mesh.devices.reshape(4, 2, 2, 4, 4), EVERY)
    split = P(EVERY)
    return jax.shard_map(
        on_device,
        mesh=fine,
        in_specs=(split, split, P(), split, split, split, split, split),
        out_specs=(split, split, P()),
        check_vma=False,
    )
```

```python
import functools
import math

import jax
import jax.numpy as jnp
import numpy as np
from jax import lax
from jax.experimental import pallas as pl
from jax.experimental.pallas import tpu as pltpu
from jax.sharding import Mesh
from jax.sharding import PartitionSpec as P

NB, C, V, TAPS = 4, 96, 512, 27
BF16, F32 = jnp.bfloat16, jnp.float32
TILE = ("y", "zh", "c")
BAND = ("zl", "x")
EVERY = TILE + BAND
PLANE = ("y", "x")
COLUMN = ("zh", "zl")
ROWS, HALF, REST = 2048, 1024, 216
MAIN = NB * V
LAT_ROWS = (C, 224, C, 160)
SCALE = 1.0 / math.sqrt(1024 * 512)
SHIFTS = [(dy, dz) for dy in range(3) for dz in range(3)]
VMEM_LIMIT = 26 * 1024 * 1024


def fill_faces(pf_ref):
    lane = lax.broadcasted_iota(jnp.int32, (1, 6 * 128), 1)
    row = lax.broadcasted_iota(jnp.int32, (V, 6 * 128), 0)
    f, p = lane >> 7, lane & 63
    first, second = p >> 3, p & 7
    on_x = 448 * f + p
    on_y = 64 * first + 56 * (f - 2) + second
    on_z = 64 * first + 8 * second + 7 * (f - 4)
    voxel = jnp.where(f < 2, on_x, jnp.where(f < 4, on_y, on_z))
    pf_ref[...] = jnp.where(row == voxel, 1.0, 0.0).astype(BF16)


def lane_low(rows):
    return lax.broadcasted_iota(jnp.int32, (rows, 128), 1) < 64


def write_faces(data, pf, send_ref, own_ref, lat_refs, zf_refs, faces_z):
    flat = data.reshape(NB * C, V)
    faces = jnp.dot(flat, pf, preferred_element_type=F32).astype(BF16)
    low = lane_low(C)
    for f in range(4):
        for b in range(NB):
            own_ref[NB * f + b] = faces[C * b : C * (b + 1), 128 * f : 128 * (f + 1)]
    for d in range(2):
        for h in range(2):
            cols = slice(128 * (4 + d), 128 * (5 + d))
            first = faces[C * 2 * h : C * (2 * h + 1), cols]
            second = faces[C * (2 * h + 1) : C * (2 * h + 2), cols]
            faces_z[d, h] = jnp.where(low, first, second)
    odd = lax.axis_index("x") & 1
    zf_refs[0][...] = faces_z[1 - odd]
    zf_refs[1][...] = faces_z[odd]
    for k in range(4):
        lat_refs[k][0:C, :] = jnp.where(low, own_ref[send_ref[0, 0, k]], own_ref[send_ref[0, 1, k]])
    for k in (1, 3):
        lat_refs[k][C:, :] = jnp.zeros((LAT_ROWS[k] - C, 128), BF16)


def fill_pool(recv_refs, pool):
    low = lane_low(C)
    odd = lax.axis_index("x") & 1

    def spread(pair, at):
        turned = pltpu.roll(pair, 64, 1)
        pool[at] = jnp.where(low, pair, turned)
        pool[at + 1] = jnp.where(low, turned, pair)

    for k in range(4):
        spread(recv_refs[k][0:C, :], 16 + 2 * k)
    for h in range(2):
        spread(recv_refs[4][h], 30 - 5 * odd + 2 * h)
        spread(recv_refs[5][h], 25 + 5 * odd + 2 * h)
    for at in (24, 29, 34):
        pool[at] = jnp.zeros((C, 128), BF16)


def fill_entries(e_ref):
    lane = lax.broadcasted_iota(jnp.int32, (1, V), 1)
    row = lax.broadcasted_iota(jnp.int32, (256, V), 0)
    x, y, z = lane >> 6, (lane >> 3) & 7, lane & 7
    for t, (dy, dz) in enumerate(SHIFTS):
        if (dy, dz) == (1, 1):
            continue
        at_y, at_z = y + (dy - 1), z + (dz - 1)
        in_y, in_z = (at_y >= 0) & (at_y < 8), (at_z >= 0) & (at_z < 8)
        from_y = jnp.where(at_y < 0, 0, 64) + 8 * x + at_z
        from_z = jnp.where(at_z < 0, 128, 192) + 8 * x + at_y
        entry = jnp.where(in_z & ~in_y, from_y, jnp.where(in_y & ~in_z, from_z, -1))
        e_ref[:, V * t : V * (t + 1)] = jnp.where(row == entry, 1.0, 0.0).astype(BF16)


def build_taps(data, pool, src_ref, down_ref, up_ref, e_ref, slabs, halo, taps):
    low = lane_low(C)
    side_x = []
    for b in range(NB):
        lat = [pool[jnp.where(src_ref[b, i] < 0, 24, src_ref[b, i])] for i in range(4)]
        below = pool[jnp.where(down_ref[b] < 0, 29, 25 + down_ref[b])]
        above = pool[jnp.where(up_ref[b] < 0, 34, 30 + up_ref[b])]
        side_x.append(jnp.where(low, lat[0], lat[1]))
        slabs[C * b : C * (b + 1), 0:128] = jnp.where(low, lat[2], lat[3])
        slabs[C * b : C * (b + 1), 128:256] = jnp.where(low, below, above)
    lanes = lax.broadcasted_iota(jnp.int32, (C, V), 1)
    lane_y, lane_z = (lanes >> 3) & 7, lanes & 7
    for t, (dy, dz) in enumerate(SHIFTS):
        rows = slice(C * t, C * (t + 1))
        step = 8 * (dy - 1) + dz - 1
        if step:
            halo[...] = jnp.dot(
                slabs[...], e_ref[:, V * t : V * (t + 1)], preferred_element_type=F32
            ).astype(BF16)
            at_y, at_z = lane_y + (dy - 1), lane_z + (dz - 1)
            inside = (at_y >= 0) & (at_y < 8) & (at_z >= 0) & (at_z < 8)
        for b in range(NB):
            if step:
                shifted = pltpu.roll(data[b], (-step) % V, 1)
                shifted = jnp.where(inside, shifted, halo[C * b : C * (b + 1), :])
                edge = pltpu.roll(side_x[b], (-step) % 128, 1)
                edge = jnp.where(inside[:, :128], edge, jnp.zeros_like(edge))
            else:
                shifted, edge = data[b], side_x[b]
            taps[rows, V * b : V * (b + 1)] = shifted
            taps[rows, MAIN + 128 * b : MAIN + 128 * (b + 1)] = edge


def convolve(w3, taps, ends, finish):
    low = lane_low(C)
    ends[...] = jnp.dot(w3[: 2 * C, :], taps[:, MAIN:], preferred_element_type=F32)
    for b in range(NB):
        y = jnp.dot(w3[...], taps[:, V * b : V * (b + 1)], preferred_element_type=F32)
        place = slice(128 * b, 128 * (b + 1))
        tiles = [slice(128 * i, 128 * (i + 1)) for i in range(4)]
        before = [ends[:C, place]] + [pltpu.roll(y[:C, tile], 64, 1) for tile in tiles]
        after = [pltpu.roll(y[C : 2 * C, tile], 64, 1) for tile in tiles] + [ends[C:, place]]
        parts = [
            y[2 * C :, tiles[i]]
            + jnp.where(low, before[i], before[i + 1])
            + jnp.where(low, after[i], after[i + 1])
            for i in range(4)
        ]
        finish(b, jnp.concatenate(parts, axis=1))


def kernel_terms(taps, delta_ref, around, terms_ref):
    low = lane_low(C)
    zero = jnp.zeros((C, 128), BF16)
    for b in range(NB):
        tiles = [delta_ref[b, :, 128 * i : 128 * (i + 1)] for i in range(4)]
        turned = [pltpu.roll(tile, 64, 1) for tile in tiles]
        for i in range(4):
            place = slice(V * b + 128 * i, V * b + 128 * (i + 1))
            around[:C, place] = jnp.where(low, turned[i], turned[i + 1] if i < 3 else zero)
            around[C:, place] = jnp.where(low, turned[i - 1] if i else zero, turned[i])
        place = slice(MAIN + 128 * b, MAIN + 128 * (b + 1))
        around[:C, place] = jnp.where(low, tiles[0], zero)
        around[C:, place] = jnp.where(low, zero, tiles[3])
    over_lanes = (((1,), (1,)), ((), ()))
    rows = 9 * C
    sides = lax.dot_general(taps[...], around[...], over_lanes, preferred_element_type=F32)
    terms_ref[0:rows, :] = sides[:, 0:128]
    terms_ref[rows : 2 * rows, 0:64] = sides[:, 128:192]
    delta = jnp.concatenate([delta_ref[b] for b in range(NB)], axis=1)
    middle = lax.dot_general(taps[:, :MAIN], delta, over_lanes, preferred_element_type=F32)
    terms_ref[rows : 2 * rows, 64:128] = middle[:, 0:64]
    for g in range(4):
        terms_ref[2 * rows : 2 * rows + REST, 32 * g : 32 * (g + 1)] = middle[
            REST * g : REST * (g + 1), 64:C
        ]
    terms_ref[2 * rows + REST :, :] = jnp.zeros((ROWS - 2 * rows - REST, 128), F32)


def masked_of(feat_ref, occ_ref):
    occ = occ_ref[...].astype(F32).astype(BF16)
    return jnp.stack([feat_ref[b] * occ[b : b + 1, :] for b in range(NB)])


def started(sems, *pairs):
    copies = [pltpu.make_async_copy(a, b, sems.at[i]) for i, (a, b) in enumerate(pairs)]
    for copy in copies:
        copy.start()
    return copies


def waited(*copies):
    for copy in copies:
        copy.wait()


def faces_kernel(feat_in, occ_in, send_in, masked_ref, own_ref, *refs):
    feat, occ, pf, send, faces_z, sems = refs[6:]
    copies = started(sems, (send_in, send), (occ_in, occ), (feat_in, feat))
    fill_faces(pf)
    waited(*copies)
    masked_ref[...] = masked_of(feat, occ)
    write_faces(masked_ref[...], pf[...], send, own_ref, refs[:4], refs[4:6], faces_z)


def delta_faces_kernel(delta_ref, send_in, *refs):
    own, pf, send, faces_z, sems = refs[6:]
    copies = started(sems, (send_in, send))
    fill_faces(pf)
    waited(*copies)
    write_faces(delta_ref[...], pf[...], send, own, refs[:4], refs[4:6], faces_z)


def delta_own_kernel(delta_in, own_out, delta, own, pf, sems):
    copies = started(sems, (delta_in, delta))
    fill_faces(pf)
    waited(*copies)
    faces = jnp.dot(delta[...].reshape(NB * C, V), pf[:, :512], preferred_element_type=F32).astype(BF16)
    for f in range(4):
        for b in range(NB):
            own[NB * f + b] = faces[C * b : C * (b + 1), 128 * f : 128 * (f + 1)]
    waited(*started(sems.at[1:], (own, own_out)))


def forward_kernel(
    feat_in, occ_in, grad_in, w_in, src_in, down_in, up_in,
    masked_ref, own_ref, recv0, recv1, recv2, recv3, recv4, recv5,
    out_out, delta_ref, keep_ref, give_ref,
    occ, grad, w, src, down, up, out, pool, slabs, halo, taps, w3, e, ends, sems, out_sems,
    feat, terms_ref, around,
):
    early = started(sems, (src_in, src), (down_in, down), (up_in, up))
    later = started(
        sems.at[3:], (w_in, w), (occ_in, occ), (feat_in, feat), (grad_in, grad)
    )
    for i in range(16):
        pool[i] = own_ref[i]
    fill_pool((recv0, recv1, recv2, recv3, recv4, recv5), pool)
    fill_entries(e)
    waited(*early)
    build_taps(masked_ref[...], pool, src, down, up, e, slabs, halo, taps)
    waited(*later)
    for i, dx in enumerate((0, 2, 1)):
        w3[C * i : C * (i + 1), :] = w[9 * dx : 9 * (dx + 1)].reshape(9 * C, C).T
    leaving = []

    def finish(b, pre):
        mask = occ[b : b + 1, :].astype(F32)
        sig = jax.nn.sigmoid(pre)
        out[b] = (feat[b].astype(F32) + mask * (pre * sig)).astype(BF16)
        leaving.extend(started(out_sems.at[b:], (out.at[b], out_out.at[b])))
        delta = grad[b].astype(F32) * mask * (sig * (1.0 + pre * (1.0 - sig)))
        delta_ref[b] = delta.astype(BF16)

    convolve(w3, taps, ends, finish)
    kernel_terms(taps, delta_ref, around, terms_ref)
    core = lax.axis_index("c")
    keep_ref[...] = terms_ref[pl.ds(pl.multiple_of(core * HALF, HALF), HALF), :]
    give_ref[...] = terms_ref[pl.ds(pl.multiple_of((1 - core) * HALF, HALF), HALF), :]
    waited(*leaving)


def backward_kernel(
    occ_in, grad_in, w_in, src_in, down_in, up_in, delta_in, own_in,
    recv0, recv1, recv2, recv3, recv4, recv5,
    out_out,
    occ, grad, w, src, down, up, out, pool, slabs, halo, taps, w3, e, ends, sems, out_sems,
    delta, lateral, vertical,
):
    early = started(
        sems,
        *[(recv.at[0:C], lateral.at[k]) for k, recv in enumerate((recv0, recv1, recv2, recv3))],
        (recv4, vertical.at[0]), (recv5, vertical.at[1]), (own_in, pool.at[0:16]),
        (src_in, src), (down_in, down), (up_in, up), (delta_in, delta),
    )
    later = started(sems.at[11:], (w_in, w), (grad_in, grad), (occ_in, occ))
    fill_entries(e)
    waited(*early)
    fill_pool([lateral.at[k] for k in range(4)] + [vertical.at[0], vertical.at[1]], pool)
    build_taps(delta[...], pool, src, down, up, e, slabs, halo, taps)
    waited(*later)
    for i, dx in enumerate((0, 2, 1)):
        last = TAPS - 1 - 9 * dx
        w3[C * i : C * (i + 1), :] = jnp.concatenate([w[last - t] for t in range(9)], axis=1)
    leaving = []

    def finish(b, back):
        mask = occ[b : b + 1, :].astype(F32)
        out[b] = (grad[b].astype(F32) + mask * back).astype(BF16)
        leaving.extend(started(out_sems.at[b:], (out.at[b], out_out.at[b])))

    convolve(w3, taps, ends, finish)
    waited(*leaving)


def sum_kernel(pieces_ref, out_ref):
    total = pieces_ref[0]
    for i in range(1, pieces_ref.shape[0]):
        total = total + pieces_ref[i]
    total = total.astype(out_ref.dtype)
    for i in range(out_ref.shape[0]):
        out_ref[i] = total


def unpack_kernel(mine_ref, other_ref, out_out, packed, out, sems):
    core = lax.axis_index("c")
    packed[pl.ds(pl.multiple_of(core * HALF, HALF), HALF), :] = mine_ref[...].astype(F32) * SCALE
    packed[pl.ds(pl.multiple_of((1 - core) * HALF, HALF), HALF), :] = other_ref[...].astype(F32) * SCALE
    rows = 9 * C
    third = [pl.ds(rows * i, rows) for i in range(3)]
    out[0:rows, :] = packed[0:rows, 0:C]
    leaving = started(sems, (out.at[third[0]], out_out.at[third[0]]))
    out[2 * rows :, 0:32] = packed[0:rows, C:128]
    out[2 * rows :, 32:C] = packed[rows : 2 * rows, 0:64]
    leaving += started(sems.at[1:], (out.at[third[2]], out_out.at[third[2]]))
    out[rows : 2 * rows, 0:64] = packed[rows : 2 * rows, 64:128]
    for g in range(4):
        out[rows + REST * g : rows + REST * (g + 1), 64:C] = packed[
            2 * rows : 2 * rows + REST, 32 * g : 32 * (g + 1)
        ]
    leaving += started(sems.at[2:], (out.at[third[1]], out_out.at[third[1]]))
    waited(*leaving)


VM = pl.BlockSpec(memory_space=pltpu.VMEM)
HB = pl.BlockSpec(memory_space=pltpu.HBM)
MIB = 1024 * 1024


def call(kernel, ins, outs, scratch=(), flops=0, moved=0, limit=8 * MIB):
    return pl.pallas_call(
        kernel,
        in_specs=ins,
        out_specs=[out[0] for out in outs],
        out_shape=[(out[3] if len(out) > 3 else jax.ShapeDtypeStruct)(out[1], out[2]) for out in outs],
        scratch_shapes=list(scratch),
        compiler_params=pltpu.CompilerParams(vmem_limit_bytes=limit),
        cost_estimate=pl.CostEstimate(flops=flops, bytes_accessed=moved, transcendentals=0),
    )


FACE_OUTS = [(VM, (16, C, 128), BF16)] + [(VM, (n, 128), BF16) for n in LAT_ROWS]
FACE_OUTS += [(VM, (2, C, 128), BF16)] * 2
BLOCKS = (NB, C, V)
FEAT, OCC = pltpu.VMEM(BLOCKS, BF16), pltpu.VMEM((NB, V), jnp.int32)
PF, SEND = pltpu.VMEM((V, 768), BF16), pltpu.SMEM((1, 2, 4), jnp.int32)
FACES_Z = pltpu.VMEM((2, 2, C, 128), BF16)
SCRATCH = [
    OCC,
    pltpu.VMEM(BLOCKS, BF16),
    pltpu.VMEM((TAPS, C, C), BF16),
    pltpu.SMEM((NB, 4), jnp.int32),
    pltpu.SMEM((NB,), jnp.int32),
    pltpu.SMEM((NB,), jnp.int32),
    pltpu.VMEM(BLOCKS, BF16),
    pltpu.VMEM((35, C, 128), BF16),
    pltpu.VMEM((NB * C, 256), BF16),
    pltpu.VMEM((NB * C, V), BF16),
    pltpu.VMEM((9 * C, MAIN + NB * 128), BF16),
    pltpu.VMEM((3 * C, 9 * C), BF16),
    pltpu.VMEM((256, 9 * V), BF16),
    pltpu.VMEM((2 * C, NB * 128), F32),
    pltpu.SemaphoreType.DMA((16,)),
    pltpu.SemaphoreType.DMA((NB,)),
]


def exchange(lat0, lat1, lat2, lat3, zf0, zf1):
    pairs = [(i, i + 1) for i in range(16)]
    flip2 = [(0, 1), (1, 0)]
    return [
        lax.ppermute(lat0, "c", flip2),
        lax.ppermute(lat1, "zh", flip2),
        lax.ppermute(lat2, "y", [(i, i ^ 1) for i in range(4)]),
        lax.ppermute(lat3, "y", [(i, i ^ 2) for i in range(4)]),
        lax.ppermute(zf0, BAND, [p for i, j in pairs[0:15:2] for p in ((i, j), (j, i))]),
        lax.ppermute(zf1, BAND, [p for i, j in pairs[1:15:2] for p in ((i, j), (j, i))]),
    ]


def exchanged(pieces, axes):
    return lax.all_to_all(pieces, axes, 0, 0, tiled=True)


def summed(pieces, count, kind):
    (out,) = call(
        sum_kernel, [VM], [(VM, (count, 64, 128), kind)], flops=pieces.size, moved=4 * pieces.size
    )(pieces)
    return out


def in_hbm(*values):
    return [pltpu.with_memory_space_constraint(value, pltpu.HBM) for value in values]


def on_device(features, occupancy, weights, grad_out, lat_src, down_src, up_src, send_faces):
    sends = send_faces.transpose(0, 2, 1)
    masked, own, *out = call(
        faces_kernel, [HB] * 3, [(VM, BLOCKS, BF16)] + FACE_OUTS,
        [FEAT, OCC, PF, SEND, FACES_Z, pltpu.SemaphoreType.DMA((3,))],
    )(*in_hbm(features, occupancy, sends))
    half = (VM, (HALF, 128), F32)
    layer_out, delta, keep, give = call(
        forward_kernel,
        [HB] * 7 + [VM] * 8,
        [(HB, BLOCKS, BF16), (VM, BLOCKS, BF16), half, half],
        SCRATCH
        + [FEAT, pltpu.VMEM((ROWS, 128), F32), pltpu.VMEM((2 * C, MAIN + NB * 128), BF16)],
        limit=VMEM_LIMIT,
    )(
        *in_hbm(features, occupancy, grad_out, weights, lat_src, down_src, up_src),
        masked,
        own,
        *exchange(*out),
    )
    out = call(
        delta_faces_kernel, [VM, HB], FACE_OUTS[1:],
        [pltpu.VMEM((16, C, 128), BF16), PF, SEND, FACES_Z, pltpu.SemaphoreType.DMA((1,))],
        flops=2 * 384 * 512 * 768, moved=2 * 10**6,
    )(delta, *in_hbm(sends))
    (delta_own,) = call(
        delta_own_kernel, [HB], [(HB, (16, C, 128), BF16, pltpu.HBM)],
        [FEAT, pltpu.VMEM((16, C, 128), BF16), PF, pltpu.SemaphoreType.DMA((2,))],
        flops=2 * 384 * 512 * 512, moved=2 * 10**6,
    )(*in_hbm(delta))
    other = lax.ppermute(give, "c", [(0, 1), (1, 0)])
    other, *out = lax.optimization_barrier((other, *out))
    halos = exchange(*out)
    part = keep + other
    part = exchanged(part.reshape(16, HALF // 16, 128), PLANE)
    part, halos[1], halos[2], halos[4] = lax.optimization_barrier((part, halos[1], halos[2], halos[4]))
    part = exchanged(summed(part, 8, F32), COLUMN)
    part, delta_own, halos[0], halos[3], halos[5] = lax.optimization_barrier(
        (part, delta_own, halos[0], halos[3], halos[5])
    )
    part = exchanged(summed(part, 16, BF16), PLANE)
    (input_grad,) = call(
        backward_kernel,
        [HB] * 14,
        [(HB, BLOCKS, BF16)],
        SCRATCH + [FEAT, pltpu.VMEM((4, C, 128), BF16), pltpu.VMEM((2, 2, C, 128), BF16)],
        flops=5 * 10**9, moved=4 * 10**6, limit=VMEM_LIMIT,
    )(
        *in_hbm(occupancy, grad_out, weights, lat_src, down_src, up_src, delta, delta_own),
        *in_hbm(*halos),
    )
    mine, input_grad = lax.optimization_barrier((part.reshape(HALF, 128), input_grad))
    other = lax.ppermute(mine, "c", [(0, 1), (1, 0)])
    (weight_grad,) = call(
        unpack_kernel, [VM, VM], [(HB, (TAPS * C, C), F32)],
        [pltpu.VMEM((ROWS, 128), F32), pltpu.VMEM((TAPS * C, C), F32), pltpu.SemaphoreType.DMA((3,))],
    )(mine, other)
    return layer_out, input_grad, weight_grad.reshape(TAPS, C, C)


def solution(mesh):
    fine = Mesh(mesh.devices.reshape(4, 2, 2, 4, 4), EVERY)
    split = P(EVERY)
    return jax.shard_map(
        on_device,
        mesh=fine,
        in_specs=(split, split, P(), split, split, split, split, split),
        out_specs=(split, split, P()),
        check_vma=False,
    )
```

```python
import functools
import math

import jax
import jax.numpy as jnp
import numpy as np
from jax import lax
from jax.experimental import pallas as pl
from jax.experimental.pallas import tpu as pltpu
from jax.sharding import Mesh
from jax.sharding import PartitionSpec as P

NB, C, V, TAPS = 4, 96, 512, 27
BF16, F32 = jnp.bfloat16, jnp.float32
TILE = ("y", "zh", "c")
BAND = ("zl", "x")
EVERY = TILE + BAND
PLANE = ("y", "x")
COLUMN = ("zh", "zl")
ROWS, HALF, REST = 2048, 1024, 216
MAIN = NB * V
LAT_ROWS = (C, 224, C, 160)
SCALE = 1.0 / math.sqrt(1024 * 512)
SHIFTS = [(dy, dz) for dy in range(3) for dz in range(3)]
VMEM_LIMIT = 26 * 1024 * 1024


def fill_faces(pf_ref):
    lane = lax.broadcasted_iota(jnp.int32, (1, 6 * 128), 1)
    row = lax.broadcasted_iota(jnp.int32, (V, 6 * 128), 0)
    f, p = lane >> 7, lane & 63
    first, second = p >> 3, p & 7
    on_x = 448 * f + p
    on_y = 64 * first + 56 * (f - 2) + second
    on_z = 64 * first + 8 * second + 7 * (f - 4)
    voxel = jnp.where(f < 2, on_x, jnp.where(f < 4, on_y, on_z))
    pf_ref[...] = jnp.where(row == voxel, 1.0, 0.0).astype(BF16)


def lane_low(rows):
    return lax.broadcasted_iota(jnp.int32, (rows, 128), 1) < 64


def write_faces(data, pf, send_ref, own_ref, lat_refs, zf_refs, faces_z):
    flat = data.reshape(NB * C, V)
    faces = jnp.dot(flat, pf, preferred_element_type=F32).astype(BF16)
    low = lane_low(C)
    for f in range(4):
        for b in range(NB):
            own_ref[NB * f + b] = faces[C * b : C * (b + 1), 128 * f : 128 * (f + 1)]
    for d in range(2):
        for h in range(2):
            cols = slice(128 * (4 + d), 128 * (5 + d))
            first = faces[C * 2 * h : C * (2 * h + 1), cols]
            second = faces[C * (2 * h + 1) : C * (2 * h + 2), cols]
            faces_z[d, h] = jnp.where(low, first, second)
    odd = lax.axis_index("x") & 1
    zf_refs[0][...] = faces_z[1 - odd]
    zf_refs[1][...] = faces_z[odd]
    for k in range(4):
        lat_refs[k][0:C, :] = jnp.where(low, own_ref[send_ref[0, 0, k]], own_ref[send_ref[0, 1, k]])
    for k in (1, 3):
        lat_refs[k][C:, :] = jnp.zeros((LAT_ROWS[k] - C, 128), BF16)


def fill_pool(recv_refs, pool):
    low = lane_low(C)
    odd = lax.axis_index("x") & 1

    def spread(pair, at):
        turned = pltpu.roll(pair, 64, 1)
        pool[at] = jnp.where(low, pair, turned)
        pool[at + 1] = jnp.where(low, turned, pair)

    for k in range(4):
        spread(recv_refs[k][0:C, :], 16 + 2 * k)
    for h in range(2):
        spread(recv_refs[4][h], 30 - 5 * odd + 2 * h)
        spread(recv_refs[5][h], 25 + 5 * odd + 2 * h)
    for at in (24, 29, 34):
        pool[at] = jnp.zeros((C, 128), BF16)


def fill_entries(e_ref):
    lane = lax.broadcasted_iota(jnp.int32, (1, V), 1)
    row = lax.broadcasted_iota(jnp.int32, (256, V), 0)
    x, y, z = lane >> 6, (lane >> 3) & 7, lane & 7
    for t, (dy, dz) in enumerate(SHIFTS):
        if (dy, dz) == (1, 1):
            continue
        at_y, at_z = y + (dy - 1), z + (dz - 1)
        in_y, in_z = (at_y >= 0) & (at_y < 8), (at_z >= 0) & (at_z < 8)
        from_y = jnp.where(at_y < 0, 0, 64) + 8 * x + at_z
        from_z = jnp.where(at_z < 0, 128, 192) + 8 * x + at_y
        entry = jnp.where(in_z & ~in_y, from_y, jnp.where(in_y & ~in_z, from_z, -1))
        e_ref[:, V * t : V * (t + 1)] = jnp.where(row == entry, 1.0, 0.0).astype(BF16)


def build_taps(data, pool, src_ref, down_ref, up_ref, e_ref, slabs, halo, taps):
    low = lane_low(C)
    side_x = []
    for b in range(NB):
        lat = [pool[jnp.where(src_ref[b, i] < 0, 24, src_ref[b, i])] for i in range(4)]
        below = pool[jnp.where(down_ref[b] < 0, 29, 25 + down_ref[b])]
        above = pool[jnp.where(up_ref[b] < 0, 34, 30 + up_ref[b])]
        side_x.append(jnp.where(low, lat[0], lat[1]))
        slabs[C * b : C * (b + 1), 0:128] = jnp.where(low, lat[2], lat[3])
        slabs[C * b : C * (b + 1), 128:256] = jnp.where(low, below, above)
    lanes = lax.broadcasted_iota(jnp.int32, (C, V), 1)
    lane_y, lane_z = (lanes >> 3) & 7, lanes & 7
    for t, (dy, dz) in enumerate(SHIFTS):
        rows = slice(C * t, C * (t + 1))
        step = 8 * (dy - 1) + dz - 1
        if step:
            halo[...] = jnp.dot(
                slabs[...], e_ref[:, V * t : V * (t + 1)], preferred_element_type=F32
            ).astype(BF16)
            at_y, at_z = lane_y + (dy - 1), lane_z + (dz - 1)
            inside = (at_y >= 0) & (at_y < 8) & (at_z >= 0) & (at_z < 8)
        for b in range(NB):
            if step:
                shifted = pltpu.roll(data[b], (-step) % V, 1)
                shifted = jnp.where(inside, shifted, halo[C * b : C * (b + 1), :])
                edge = pltpu.roll(side_x[b], (-step) % 128, 1)
                edge = jnp.where(inside[:, :128], edge, jnp.zeros_like(edge))
            else:
                shifted, edge = data[b], side_x[b]
            taps[rows, V * b : V * (b + 1)] = shifted
            taps[rows, MAIN + 128 * b : MAIN + 128 * (b + 1)] = edge


def convolve(w3, taps, ends, finish):
    low = lane_low(C)
    ends[...] = jnp.dot(w3[: 2 * C, :], taps[:, MAIN:], preferred_element_type=F32)
    for b in range(NB):
        y = jnp.dot(w3[...], taps[:, V * b : V * (b + 1)], preferred_element_type=F32)
        place = slice(128 * b, 128 * (b + 1))
        tiles = [slice(128 * i, 128 * (i + 1)) for i in range(4)]
        before = [ends[:C, place]] + [pltpu.roll(y[:C, tile], 64, 1) for tile in tiles]
        after = [pltpu.roll(y[C : 2 * C, tile], 64, 1) for tile in tiles] + [ends[C:, place]]
        parts = [
            y[2 * C :, tiles[i]]
            + jnp.where(low, before[i], before[i + 1])
            + jnp.where(low, after[i], after[i + 1])
            for i in range(4)
        ]
        finish(b, jnp.concatenate(parts, axis=1))


def kernel_terms(taps, delta_ref, around, terms_ref):
    low = lane_low(C)
    zero = jnp.zeros((C, 128), BF16)
    for b in range(NB):
        tiles = [delta_ref[b, :, 128 * i : 128 * (i + 1)] for i in range(4)]
        turned = [pltpu.roll(tile, 64, 1) for tile in tiles]
        for i in range(4):
            place = slice(V * b + 128 * i, V * b + 128 * (i + 1))
            around[:C, place] = jnp.where(low, turned[i], turned[i + 1] if i < 3 else zero)
            around[C:, place] = jnp.where(low, turned[i - 1] if i else zero, turned[i])
        place = slice(MAIN + 128 * b, MAIN + 128 * (b + 1))
        around[:C, place] = jnp.where(low, tiles[0], zero)
        around[C:, place] = jnp.where(low, zero, tiles[3])
    over_lanes = (((1,), (1,)), ((), ()))
    rows = 9 * C
    sides = lax.dot_general(taps[...], around[...], over_lanes, preferred_element_type=F32)
    terms_ref[0:rows, :] = sides[:, 0:128]
    terms_ref[rows : 2 * rows, 0:64] = sides[:, 128:192]
    delta = jnp.concatenate([delta_ref[b] for b in range(NB)], axis=1)
    middle = lax.dot_general(taps[:, :MAIN], delta, over_lanes, preferred_element_type=F32)
    terms_ref[rows : 2 * rows, 64:128] = middle[:, 0:64]
    for g in range(4):
        terms_ref[2 * rows : 2 * rows + REST, 32 * g : 32 * (g + 1)] = middle[
            REST * g : REST * (g + 1), 64:C
        ]
    terms_ref[2 * rows + REST :, :] = jnp.zeros((ROWS - 2 * rows - REST, 128), F32)


def masked_of(feat_ref, occ_ref):
    occ = occ_ref[...].astype(F32).astype(BF16)
    return jnp.stack([feat_ref[b] * occ[b : b + 1, :] for b in range(NB)])


def started(sems, *pairs):
    copies = [pltpu.make_async_copy(a, b, sems.at[i]) for i, (a, b) in enumerate(pairs)]
    for copy in copies:
        copy.start()
    return copies


def waited(*copies):
    for copy in copies:
        copy.wait()


def faces_kernel(feat_in, occ_in, send_in, masked_ref, own_ref, *refs):
    feat, occ, pf, send, faces_z, sems = refs[6:]
    copies = started(sems, (send_in, send), (occ_in, occ), (feat_in, feat))
    fill_faces(pf)
    waited(*copies)
    masked_ref[...] = masked_of(feat, occ)
    write_faces(masked_ref[...], pf[...], send, own_ref, refs[:4], refs[4:6], faces_z)


def delta_faces_kernel(delta_ref, send_in, *refs):
    own, pf, send, faces_z, sems = refs[6:]
    copies = started(sems, (send_in, send))
    fill_faces(pf)
    waited(*copies)
    write_faces(delta_ref[...], pf[...], send, own, refs[:4], refs[4:6], faces_z)


def delta_own_kernel(delta_in, own_out, delta, own, pf, sems):
    copies = started(sems, (delta_in, delta))
    fill_faces(pf)
    waited(*copies)
    faces = jnp.dot(delta[...].reshape(NB * C, V), pf[:, :512], preferred_element_type=F32).astype(BF16)
    for f in range(4):
        for b in range(NB):
            own[NB * f + b] = faces[C * b : C * (b + 1), 128 * f : 128 * (f + 1)]
    waited(*started(sems.at[1:], (own, own_out)))


def forward_kernel(
    feat_in, occ_in, grad_in, w_in, src_in, down_in, up_in,
    masked_ref, own_ref, recv0, recv1, recv2, recv3, recv4, recv5,
    out_out, delta_ref, keep_ref, give_ref,
    occ, grad, w, src, down, up, out, pool, slabs, halo, taps, w3, e, ends, sems, out_sems,
    feat, terms_ref, around,
):
    early = started(sems, (src_in, src), (down_in, down), (up_in, up))
    later = started(
        sems.at[3:], (w_in, w), (occ_in, occ), (feat_in, feat), (grad_in, grad)
    )
    for i in range(16):
        pool[i] = own_ref[i]
    fill_pool((recv0, recv1, recv2, recv3, recv4, recv5), pool)
    fill_entries(e)
    waited(*early)
    build_taps(masked_ref[...], pool, src, down, up, e, slabs, halo, taps)
    waited(*later)
    for i, dx in enumerate((0, 2, 1)):
        w3[C * i : C * (i + 1), :] = w[9 * dx : 9 * (dx + 1)].reshape(9 * C, C).T
    leaving = []

    def finish(b, pre):
        mask = occ[b : b + 1, :].astype(F32)
        sig = jax.nn.sigmoid(pre)
        out[b] = (feat[b].astype(F32) + mask * (pre * sig)).astype(BF16)
        leaving.extend(started(out_sems.at[b:], (out.at[b], out_out.at[b])))
        delta = grad[b].astype(F32) * mask * (sig * (1.0 + pre * (1.0 - sig)))
        delta_ref[b] = delta.astype(BF16)

    convolve(w3, taps, ends, finish)
    kernel_terms(taps, delta_ref, around, terms_ref)
    core = lax.axis_index("c")
    keep_ref[...] = terms_ref[pl.ds(pl.multiple_of(core * HALF, HALF), HALF), :]
    give_ref[...] = terms_ref[pl.ds(pl.multiple_of((1 - core) * HALF, HALF), HALF), :]
    waited(*leaving)


def backward_kernel(
    occ_in, grad_in, w_in, src_in, down_in, up_in, delta_in, own_in,
    recv0, recv1, recv2, recv3, recv4, recv5,
    out_out,
    occ, grad, w, src, down, up, out, pool, slabs, halo, taps, w3, e, ends, sems, out_sems,
    delta, lateral, vertical,
):
    early = started(
        sems,
        *[(recv.at[0:C], lateral.at[k]) for k, recv in enumerate((recv0, recv1, recv2, recv3))],
        (recv4, vertical.at[0]), (recv5, vertical.at[1]), (own_in, pool.at[0:16]),
        (src_in, src), (down_in, down), (up_in, up), (delta_in, delta),
    )
    later = started(sems.at[11:], (w_in, w), (grad_in, grad), (occ_in, occ))
    fill_entries(e)
    waited(*early)
    fill_pool([lateral.at[k] for k in range(4)] + [vertical.at[0], vertical.at[1]], pool)
    build_taps(delta[...], pool, src, down, up, e, slabs, halo, taps)
    waited(*later)
    for i, dx in enumerate((0, 2, 1)):
        last = TAPS - 1 - 9 * dx
        w3[C * i : C * (i + 1), :] = jnp.concatenate([w[last - t] for t in range(9)], axis=1)
    leaving = []

    def finish(b, back):
        mask = occ[b : b + 1, :].astype(F32)
        out[b] = (grad[b].astype(F32) + mask * back).astype(BF16)
        leaving.extend(started(out_sems.at[b:], (out.at[b], out_out.at[b])))

    convolve(w3, taps, ends, finish)
    waited(*leaving)


def sum_kernel(pieces_ref, out_ref):
    total = pieces_ref[0]
    for i in range(1, pieces_ref.shape[0]):
        total = total + pieces_ref[i]
    total = total.astype(out_ref.dtype)
    for i in range(out_ref.shape[0]):
        out_ref[i] = total


def unpack_kernel(mine_ref, other_ref, out_out, packed, out, sems):
    core = lax.axis_index("c")
    packed[pl.ds(pl.multiple_of(core * HALF, HALF), HALF), :] = mine_ref[...].astype(F32) * SCALE
    packed[pl.ds(pl.multiple_of((1 - core) * HALF, HALF), HALF), :] = other_ref[...].astype(F32) * SCALE
    rows = 9 * C
    third = [pl.ds(rows * i, rows) for i in range(3)]
    out[0:rows, :] = packed[0:rows, 0:C]
    leaving = started(sems, (out.at[third[0]], out_out.at[third[0]]))
    out[2 * rows :, 0:32] = packed[0:rows, C:128]
    out[2 * rows :, 32:C] = packed[rows : 2 * rows, 0:64]
    leaving += started(sems.at[1:], (out.at[third[2]], out_out.at[third[2]]))
    out[rows : 2 * rows, 0:64] = packed[rows : 2 * rows, 64:128]
    for g in range(4):
        out[rows + REST * g : rows + REST * (g + 1), 64:C] = packed[
            2 * rows : 2 * rows + REST, 32 * g : 32 * (g + 1)
        ]
    leaving += started(sems.at[2:], (out.at[third[1]], out_out.at[third[1]]))
    waited(*leaving)


VM = pl.BlockSpec(memory_space=pltpu.VMEM)
HB = pl.BlockSpec(memory_space=pltpu.HBM)
MIB = 1024 * 1024


def call(kernel, ins, outs, scratch=(), flops=0, moved=0, limit=8 * MIB):
    return pl.pallas_call(
        kernel,
        in_specs=ins,
        out_specs=[out[0] for out in outs],
        out_shape=[(out[3] if len(out) > 3 else jax.ShapeDtypeStruct)(out[1], out[2]) for out in outs],
        scratch_shapes=list(scratch),
        compiler_params=pltpu.CompilerParams(vmem_limit_bytes=limit),
        cost_estimate=pl.CostEstimate(flops=flops, bytes_accessed=moved, transcendentals=0),
    )


FACE_OUTS = [(VM, (16, C, 128), BF16)] + [(VM, (n, 128), BF16) for n in LAT_ROWS]
FACE_OUTS += [(VM, (2, C, 128), BF16)] * 2
BLOCKS = (NB, C, V)
FEAT, OCC = pltpu.VMEM(BLOCKS, BF16), pltpu.VMEM((NB, V), jnp.int32)
PF, SEND = pltpu.VMEM((V, 768), BF16), pltpu.SMEM((1, 2, 4), jnp.int32)
FACES_Z = pltpu.VMEM((2, 2, C, 128), BF16)
SCRATCH = [
    OCC,
    pltpu.VMEM(BLOCKS, BF16),
    pltpu.VMEM((TAPS, C, C), BF16),
    pltpu.SMEM((NB, 4), jnp.int32),
    pltpu.SMEM((NB,), jnp.int32),
    pltpu.SMEM((NB,), jnp.int32),
    pltpu.VMEM(BLOCKS, BF16),
    pltpu.VMEM((35, C, 128), BF16),
    pltpu.VMEM((NB * C, 256), BF16),
    pltpu.VMEM((NB * C, V), BF16),
    pltpu.VMEM((9 * C, MAIN + NB * 128), BF16),
    pltpu.VMEM((3 * C, 9 * C), BF16),
    pltpu.VMEM((256, 9 * V), BF16),
    pltpu.VMEM((2 * C, NB * 128), F32),
    pltpu.SemaphoreType.DMA((16,)),
    pltpu.SemaphoreType.DMA((NB,)),
]


def exchange(lat0, lat1, lat2, lat3, zf0, zf1):
    pairs = [(i, i + 1) for i in range(16)]
    flip2 = [(0, 1), (1, 0)]
    return [
        lax.ppermute(lat0, "c", flip2),
        lax.ppermute(lat1, "zh", flip2),
        lax.ppermute(lat2, "y", [(i, i ^ 1) for i in range(4)]),
        lax.ppermute(lat3, "y", [(i, i ^ 2) for i in range(4)]),
        lax.ppermute(zf0, BAND, [p for i, j in pairs[0:15:2] for p in ((i, j), (j, i))]),
        lax.ppermute(zf1, BAND, [p for i, j in pairs[1:15:2] for p in ((i, j), (j, i))]),
    ]


def exchanged(pieces, axes):
    return lax.all_to_all(pieces, axes, 0, 0, tiled=True)


def summed(pieces, count, kind):
    (out,) = call(
        sum_kernel, [VM], [(VM, (count, 64, 128), kind)], flops=pieces.size, moved=4 * pieces.size
    )(pieces)
    return out


def in_hbm(*values):
    return [pltpu.with_memory_space_constraint(value, pltpu.HBM) for value in values]


def on_device(features, occupancy, weights, grad_out, lat_src, down_src, up_src, send_faces):
    sends = send_faces.transpose(0, 2, 1)
    masked, own, *out = call(
        faces_kernel, [HB] * 3, [(VM, BLOCKS, BF16)] + FACE_OUTS,
        [FEAT, OCC, PF, SEND, FACES_Z, pltpu.SemaphoreType.DMA((3,))],
    )(*in_hbm(features, occupancy, sends))
    half = (VM, (HALF, 128), F32)
    layer_out, delta, keep, give = call(
        forward_kernel,
        [HB] * 7 + [VM] * 8,
        [(HB, BLOCKS, BF16), (VM, BLOCKS, BF16), half, half],
        SCRATCH
        + [FEAT, pltpu.VMEM((ROWS, 128), F32), pltpu.VMEM((2 * C, MAIN + NB * 128), BF16)],
        limit=VMEM_LIMIT,
    )(
        *in_hbm(features, occupancy, grad_out, weights, lat_src, down_src, up_src),
        masked,
        own,
        *exchange(*out),
    )
    out = call(
        delta_faces_kernel, [VM, HB], FACE_OUTS[1:],
        [pltpu.VMEM((16, C, 128), BF16), PF, SEND, FACES_Z, pltpu.SemaphoreType.DMA((1,))],
        flops=2 * 384 * 512 * 768, moved=2 * 10**6,
    )(delta, *in_hbm(sends))
    (delta_own,) = call(
        delta_own_kernel, [HB], [(HB, (16, C, 128), BF16, pltpu.HBM)],
        [FEAT, pltpu.VMEM((16, C, 128), BF16), PF, pltpu.SemaphoreType.DMA((2,))],
        flops=2 * 384 * 512 * 512, moved=2 * 10**6,
    )(*in_hbm(delta))
    other = lax.ppermute(give, "c", [(0, 1), (1, 0)])
    other, *out = lax.optimization_barrier((other, *out))
    halos = exchange(*out)
    part = keep + other
    part = exchanged(part.reshape(16, HALF // 16, 128), PLANE)
    part, delta_own, halos[1], halos[2], halos[4] = lax.optimization_barrier(
        (part, delta_own, halos[1], halos[2], halos[4])
    )
    part = exchanged(summed(part, 8, F32), COLUMN)
    part, halos[0], halos[3], halos[5] = lax.optimization_barrier(
        (part, halos[0], halos[3], halos[5])
    )
    part = exchanged(summed(part, 16, BF16), PLANE)
    (input_grad,) = call(
        backward_kernel,
        [HB] * 14,
        [(HB, BLOCKS, BF16)],
        SCRATCH + [FEAT, pltpu.VMEM((4, C, 128), BF16), pltpu.VMEM((2, 2, C, 128), BF16)],
        flops=5 * 10**9, moved=4 * 10**6, limit=VMEM_LIMIT,
    )(
        *in_hbm(occupancy, grad_out, weights, lat_src, down_src, up_src, delta, delta_own),
        *in_hbm(*halos),
    )
    mine, input_grad = lax.optimization_barrier((part.reshape(HALF, 128), input_grad))
    other = lax.ppermute(mine, "c", [(0, 1), (1, 0)])
    (weight_grad,) = call(
        unpack_kernel, [VM, VM], [(HB, (TAPS * C, C), F32)],
        [pltpu.VMEM((ROWS, 128), F32), pltpu.VMEM((TAPS * C, C), F32), pltpu.SemaphoreType.DMA((3,))],
    )(mine, other)
    return layer_out, input_grad, weight_grad.reshape(TAPS, C, C)


def solution(mesh):
    fine = Mesh(mesh.devices.reshape(4, 2, 2, 4, 4), EVERY)
    split = P(EVERY)
    return jax.shard_map(
        on_device,
        mesh=fine,
        in_specs=(split, split, P(), split, split, split, split, split),
        out_specs=(split, split, P()),
        check_vma=False,
    )
```

```python
import functools
import math

import jax
import jax.numpy as jnp
import numpy as np
from jax import lax
from jax.experimental import pallas as pl
from jax.experimental.pallas import tpu as pltpu
from jax.sharding import Mesh
from jax.sharding import PartitionSpec as P

NB, C, V, TAPS = 4, 96, 512, 27
BF16, F32 = jnp.bfloat16, jnp.float32
TILE = ("y", "zh", "c")
BAND = ("zl", "x")
EVERY = TILE + BAND
PLANE = ("y", "x")
COLUMN = ("zh", "zl")
ROWS, HALF, REST = 2048, 1024, 216
MAIN = NB * V
LAT_ROWS = (C, 224, C, 160)
SCALE = 1.0 / math.sqrt(1024 * 512)
SHIFTS = [(dy, dz) for dy in range(3) for dz in range(3)]
VMEM_LIMIT = 26 * 1024 * 1024


def fill_faces(pf_ref):
    lane = lax.broadcasted_iota(jnp.int32, (1, 6 * 128), 1)
    row = lax.broadcasted_iota(jnp.int32, (V, 6 * 128), 0)
    f, p = lane >> 7, lane & 63
    first, second = p >> 3, p & 7
    on_x = 448 * f + p
    on_y = 64 * first + 56 * (f - 2) + second
    on_z = 64 * first + 8 * second + 7 * (f - 4)
    voxel = jnp.where(f < 2, on_x, jnp.where(f < 4, on_y, on_z))
    pf_ref[...] = jnp.where(row == voxel, 1.0, 0.0).astype(BF16)


def lane_low(rows):
    return lax.broadcasted_iota(jnp.int32, (rows, 128), 1) < 64


def write_faces(data, pf, send_ref, own_ref, lat_refs, zf_refs, faces_z):
    flat = data.reshape(NB * C, V)
    faces = jnp.dot(flat, pf, preferred_element_type=F32).astype(BF16)
    low = lane_low(C)
    for f in range(4):
        for b in range(NB):
            own_ref[NB * f + b] = faces[C * b : C * (b + 1), 128 * f : 128 * (f + 1)]
    for d in range(2):
        for h in range(2):
            cols = slice(128 * (4 + d), 128 * (5 + d))
            first = faces[C * 2 * h : C * (2 * h + 1), cols]
            second = faces[C * (2 * h + 1) : C * (2 * h + 2), cols]
            faces_z[d, h] = jnp.where(low, first, second)
    odd = lax.axis_index("x") & 1
    zf_refs[0][...] = faces_z[1 - odd]
    zf_refs[1][...] = faces_z[odd]
    for k in range(4):
        lat_refs[k][0:C, :] = jnp.where(low, own_ref[send_ref[0, 0, k]], own_ref[send_ref[0, 1, k]])
    for k in (1, 3):
        lat_refs[k][C:, :] = jnp.zeros((LAT_ROWS[k] - C, 128), BF16)


def fill_pool(recv_refs, pool):
    low = lane_low(C)
    odd = lax.axis_index("x") & 1

    def spread(pair, at):
        turned = pltpu.roll(pair, 64, 1)
        pool[at] = jnp.where(low, pair, turned)
        pool[at + 1] = jnp.where(low, turned, pair)

    for k in range(4):
        spread(recv_refs[k][0:C, :], 16 + 2 * k)
    for h in range(2):
        spread(recv_refs[4][h], 30 - 5 * odd + 2 * h)
        spread(recv_refs[5][h], 25 + 5 * odd + 2 * h)
    for at in (24, 29, 34):
        pool[at] = jnp.zeros((C, 128), BF16)


def fill_entries(e_ref):
    lane = lax.broadcasted_iota(jnp.int32, (1, V), 1)
    row = lax.broadcasted_iota(jnp.int32, (256, V), 0)
    x, y, z = lane >> 6, (lane >> 3) & 7, lane & 7
    for t, (dy, dz) in enumerate(SHIFTS):
        if (dy, dz) == (1, 1):
            continue
        at_y, at_z = y + (dy - 1), z + (dz - 1)
        in_y, in_z = (at_y >= 0) & (at_y < 8), (at_z >= 0) & (at_z < 8)
        from_y = jnp.where(at_y < 0, 0, 64) + 8 * x + at_z
        from_z = jnp.where(at_z < 0, 128, 192) + 8 * x + at_y
        entry = jnp.where(in_z & ~in_y, from_y, jnp.where(in_y & ~in_z, from_z, -1))
        e_ref[:, V * t : V * (t + 1)] = jnp.where(row == entry, 1.0, 0.0).astype(BF16)


def build_taps(data, pool, src_ref, down_ref, up_ref, e_ref, slabs, halo, taps):
    low = lane_low(C)
    side_x = []
    for b in range(NB):
        lat = [pool[jnp.where(src_ref[b, i] < 0, 24, src_ref[b, i])] for i in range(4)]
        below = pool[jnp.where(down_ref[b] < 0, 29, 25 + down_ref[b])]
        above = pool[jnp.where(up_ref[b] < 0, 34, 30 + up_ref[b])]
        side_x.append(jnp.where(low, lat[0], lat[1]))
        slabs[C * b : C * (b + 1), 0:128] = jnp.where(low, lat[2], lat[3])
        slabs[C * b : C * (b + 1), 128:256] = jnp.where(low, below, above)
    lanes = lax.broadcasted_iota(jnp.int32, (C, V), 1)
    lane_y, lane_z = (lanes >> 3) & 7, lanes & 7
    for t, (dy, dz) in enumerate(SHIFTS):
        rows = slice(C * t, C * (t + 1))
        step = 8 * (dy - 1) + dz - 1
        if step:
            halo[...] = jnp.dot(
                slabs[...], e_ref[:, V * t : V * (t + 1)], preferred_element_type=F32
            ).astype(BF16)
            at_y, at_z = lane_y + (dy - 1), lane_z + (dz - 1)
            inside = (at_y >= 0) & (at_y < 8) & (at_z >= 0) & (at_z < 8)
        for b in range(NB):
            if step:
                shifted = pltpu.roll(data[b], (-step) % V, 1)
                shifted = jnp.where(inside, shifted, halo[C * b : C * (b + 1), :])
                edge = pltpu.roll(side_x[b], (-step) % 128, 1)
                edge = jnp.where(inside[:, :128], edge, jnp.zeros_like(edge))
            else:
                shifted, edge = data[b], side_x[b]
            taps[rows, V * b : V * (b + 1)] = shifted
            taps[rows, MAIN + 128 * b : MAIN + 128 * (b + 1)] = edge


def convolve(w3, taps, ends, finish):
    low = lane_low(C)
    ends[...] = jnp.dot(w3[: 2 * C, :], taps[:, MAIN:], preferred_element_type=F32)
    for b in range(NB):
        y = jnp.dot(w3[...], taps[:, V * b : V * (b + 1)], preferred_element_type=F32)
        place = slice(128 * b, 128 * (b + 1))
        tiles = [slice(128 * i, 128 * (i + 1)) for i in range(4)]
        before = [ends[:C, place]] + [pltpu.roll(y[:C, tile], 64, 1) for tile in tiles]
        after = [pltpu.roll(y[C : 2 * C, tile], 64, 1) for tile in tiles] + [ends[C:, place]]
        parts = [
            y[2 * C :, tiles[i]]
            + jnp.where(low, before[i], before[i + 1])
            + jnp.where(low, after[i], after[i + 1])
            for i in range(4)
        ]
        finish(b, jnp.concatenate(parts, axis=1))


def kernel_terms(taps, delta_ref, around, terms_ref):
    low = lane_low(C)
    zero = jnp.zeros((C, 128), BF16)
    for b in range(NB):
        tiles = [delta_ref[b, :, 128 * i : 128 * (i + 1)] for i in range(4)]
        turned = [pltpu.roll(tile, 64, 1) for tile in tiles]
        for i in range(4):
            place = slice(V * b + 128 * i, V * b + 128 * (i + 1))
            around[:C, place] = jnp.where(low, turned[i], turned[i + 1] if i < 3 else zero)
            around[C:, place] = jnp.where(low, turned[i - 1] if i else zero, turned[i])
        place = slice(MAIN + 128 * b, MAIN + 128 * (b + 1))
        around[:C, place] = jnp.where(low, tiles[0], zero)
        around[C:, place] = jnp.where(low, zero, tiles[3])
    over_lanes = (((1,), (1,)), ((), ()))
    rows = 9 * C
    sides = lax.dot_general(taps[...], around[...], over_lanes, preferred_element_type=F32)
    terms_ref[0:rows, :] = sides[:, 0:128]
    terms_ref[rows : 2 * rows, 0:64] = sides[:, 128:192]
    delta = jnp.concatenate([delta_ref[b] for b in range(NB)], axis=1)
    middle = lax.dot_general(taps[:, :MAIN], delta, over_lanes, preferred_element_type=F32)
    terms_ref[rows : 2 * rows, 64:128] = middle[:, 0:64]
    for g in range(4):
        terms_ref[2 * rows : 2 * rows + REST, 32 * g : 32 * (g + 1)] = middle[
            REST * g : REST * (g + 1), 64:C
        ]
    terms_ref[2 * rows + REST :, :] = jnp.zeros((ROWS - 2 * rows - REST, 128), F32)


def masked_of(feat_ref, occ_ref):
    occ = occ_ref[...].astype(F32).astype(BF16)
    return jnp.stack([feat_ref[b] * occ[b : b + 1, :] for b in range(NB)])


def started(sems, *pairs):
    copies = [pltpu.make_async_copy(a, b, sems.at[i]) for i, (a, b) in enumerate(pairs)]
    for copy in copies:
        copy.start()
    return copies


def waited(*copies):
    for copy in copies:
        copy.wait()


def faces_kernel(feat_in, occ_in, send_in, masked_ref, own_ref, *refs):
    feat, occ, pf, send, faces_z, sems = refs[6:]
    copies = started(sems, (send_in, send), (occ_in, occ), (feat_in, feat))
    fill_faces(pf)
    waited(*copies)
    masked_ref[...] = masked_of(feat, occ)
    write_faces(masked_ref[...], pf[...], send, own_ref, refs[:4], refs[4:6], faces_z)


def delta_faces_kernel(delta_ref, send_in, *refs):
    own, pf, send, faces_z, sems = refs[6:]
    copies = started(sems, (send_in, send))
    fill_faces(pf)
    waited(*copies)
    write_faces(delta_ref[...], pf[...], send, own, refs[:4], refs[4:6], faces_z)


def delta_own_kernel(delta_in, own_out, delta, own, pf, sems):
    copies = started(sems, (delta_in, delta))
    fill_faces(pf)
    waited(*copies)
    faces = jnp.dot(delta[...].reshape(NB * C, V), pf[:, :512], preferred_element_type=F32).astype(BF16)
    for f in range(4):
        for b in range(NB):
            own[NB * f + b] = faces[C * b : C * (b + 1), 128 * f : 128 * (f + 1)]
    waited(*started(sems.at[1:], (own, own_out)))


def forward_kernel(
    feat_in, occ_in, grad_in, w_in, src_in, down_in, up_in,
    masked_ref, own_ref, recv0, recv1, recv2, recv3, recv4, recv5,
    out_out, delta_ref, keep_ref, give_ref,
    occ, grad, w, src, down, up, out, pool, slabs, halo, taps, w3, e, ends, sems, out_sems,
    feat, terms_ref, around,
):
    early = started(sems, (src_in, src), (down_in, down), (up_in, up))
    later = started(
        sems.at[3:], (w_in, w), (occ_in, occ), (feat_in, feat), (grad_in, grad)
    )
    for i in range(16):
        pool[i] = own_ref[i]
    fill_pool((recv0, recv1, recv2, recv3, recv4, recv5), pool)
    fill_entries(e)
    waited(*early)
    build_taps(masked_ref[...], pool, src, down, up, e, slabs, halo, taps)
    waited(*later)
    for i, dx in enumerate((0, 2, 1)):
        w3[C * i : C * (i + 1), :] = w[9 * dx : 9 * (dx + 1)].reshape(9 * C, C).T
    leaving = []

    def finish(b, pre):
        mask = occ[b : b + 1, :].astype(F32)
        sig = jax.nn.sigmoid(pre)
        out[b] = (feat[b].astype(F32) + mask * (pre * sig)).astype(BF16)
        leaving.extend(started(out_sems.at[b:], (out.at[b], out_out.at[b])))
        delta = grad[b].astype(F32) * mask * (sig * (1.0 + pre * (1.0 - sig)))
        delta_ref[b] = delta.astype(BF16)

    convolve(w3, taps, ends, finish)
    kernel_terms(taps, delta_ref, around, terms_ref)
    core = lax.axis_index("c")
    keep_ref[...] = terms_ref[pl.ds(pl.multiple_of(core * HALF, HALF), HALF), :]
    give_ref[...] = terms_ref[pl.ds(pl.multiple_of((1 - core) * HALF, HALF), HALF), :]
    waited(*leaving)


def backward_kernel(
    occ_in, grad_in, w_in, src_in, down_in, up_in, delta_in, own_in,
    recv0, recv1, recv2, recv3, recv4, recv5,
    out_out,
    occ, grad, w, src, down, up, out, pool, slabs, halo, taps, w3, e, ends, sems, out_sems,
    delta, lateral, vertical,
):
    early = started(
        sems,
        *[(recv.at[0:C], lateral.at[k]) for k, recv in enumerate((recv0, recv1, recv2, recv3))],
        (recv4, vertical.at[0]), (recv5, vertical.at[1]), (own_in, pool.at[0:16]),
        (src_in, src), (down_in, down), (up_in, up), (delta_in, delta),
    )
    later = started(sems.at[11:], (w_in, w), (grad_in, grad), (occ_in, occ))
    fill_entries(e)
    waited(*early)
    fill_pool([lateral.at[k] for k in range(4)] + [vertical.at[0], vertical.at[1]], pool)
    build_taps(delta[...], pool, src, down, up, e, slabs, halo, taps)
    waited(*later)
    for i, dx in enumerate((0, 2, 1)):
        last = TAPS - 1 - 9 * dx
        w3[C * i : C * (i + 1), :] = jnp.concatenate([w[last - t] for t in range(9)], axis=1)
    leaving = []

    def finish(b, back):
        mask = occ[b : b + 1, :].astype(F32)
        out[b] = (grad[b].astype(F32) + mask * back).astype(BF16)
        leaving.extend(started(out_sems.at[b:], (out.at[b], out_out.at[b])))

    convolve(w3, taps, ends, finish)
    waited(*leaving)


def sum_kernel(pieces_ref, out_ref):
    total = pieces_ref[0]
    for i in range(1, pieces_ref.shape[0]):
        total = total + pieces_ref[i]
    total = total.astype(out_ref.dtype)
    for i in range(out_ref.shape[0]):
        out_ref[i] = total


def unpack_kernel(mine_ref, other_ref, out_out, packed, out, sems):
    core = lax.axis_index("c")
    packed[pl.ds(pl.multiple_of(core * HALF, HALF), HALF), :] = mine_ref[...].astype(F32) * SCALE
    packed[pl.ds(pl.multiple_of((1 - core) * HALF, HALF), HALF), :] = other_ref[...].astype(F32) * SCALE
    rows = 9 * C
    third = [pl.ds(rows * i, rows) for i in range(3)]
    out[0:rows, :] = packed[0:rows, 0:C]
    leaving = started(sems, (out.at[third[0]], out_out.at[third[0]]))
    out[2 * rows :, 0:32] = packed[0:rows, C:128]
    out[2 * rows :, 32:C] = packed[rows : 2 * rows, 0:64]
    leaving += started(sems.at[1:], (out.at[third[2]], out_out.at[third[2]]))
    out[rows : 2 * rows, 0:64] = packed[rows : 2 * rows, 64:128]
    for g in range(4):
        out[rows + REST * g : rows + REST * (g + 1), 64:C] = packed[
            2 * rows : 2 * rows + REST, 32 * g : 32 * (g + 1)
        ]
    leaving += started(sems.at[2:], (out.at[third[1]], out_out.at[third[1]]))
    waited(*leaving)


VM = pl.BlockSpec(memory_space=pltpu.VMEM)
HB = pl.BlockSpec(memory_space=pltpu.HBM)
MIB = 1024 * 1024


def call(kernel, ins, outs, scratch=(), flops=0, moved=0, limit=8 * MIB):
    return pl.pallas_call(
        kernel,
        in_specs=ins,
        out_specs=[out[0] for out in outs],
        out_shape=[(out[3] if len(out) > 3 else jax.ShapeDtypeStruct)(out[1], out[2]) for out in outs],
        scratch_shapes=list(scratch),
        compiler_params=pltpu.CompilerParams(vmem_limit_bytes=limit),
        cost_estimate=pl.CostEstimate(flops=flops, bytes_accessed=moved, transcendentals=0),
    )


FACE_OUTS = [(VM, (16, C, 128), BF16)] + [(VM, (n, 128), BF16) for n in LAT_ROWS]
FACE_OUTS += [(VM, (2, C, 128), BF16)] * 2
BLOCKS = (NB, C, V)
FEAT, OCC = pltpu.VMEM(BLOCKS, BF16), pltpu.VMEM((NB, V), jnp.int32)
PF, SEND = pltpu.VMEM((V, 768), BF16), pltpu.SMEM((1, 2, 4), jnp.int32)
FACES_Z = pltpu.VMEM((2, 2, C, 128), BF16)
SCRATCH = [
    OCC,
    pltpu.VMEM(BLOCKS, BF16),
    pltpu.VMEM((TAPS, C, C), BF16),
    pltpu.SMEM((NB, 4), jnp.int32),
    pltpu.SMEM((NB,), jnp.int32),
    pltpu.SMEM((NB,), jnp.int32),
    pltpu.VMEM(BLOCKS, BF16),
    pltpu.VMEM((35, C, 128), BF16),
    pltpu.VMEM((NB * C, 256), BF16),
    pltpu.VMEM((NB * C, V), BF16),
    pltpu.VMEM((9 * C, MAIN + NB * 128), BF16),
    pltpu.VMEM((3 * C, 9 * C), BF16),
    pltpu.VMEM((256, 9 * V), BF16),
    pltpu.VMEM((2 * C, NB * 128), F32),
    pltpu.SemaphoreType.DMA((16,)),
    pltpu.SemaphoreType.DMA((NB,)),
]


def exchange(lat0, lat1, lat2, lat3, zf0, zf1):
    pairs = [(i, i + 1) for i in range(16)]
    flip2 = [(0, 1), (1, 0)]
    return [
        lax.ppermute(lat0, "c", flip2),
        lax.ppermute(lat1, "zh", flip2),
        lax.ppermute(lat2, "y", [(i, i ^ 1) for i in range(4)]),
        lax.ppermute(lat3, "y", [(i, i ^ 2) for i in range(4)]),
        lax.ppermute(zf0, BAND, [p for i, j in pairs[0:15:2] for p in ((i, j), (j, i))]),
        lax.ppermute(zf1, BAND, [p for i, j in pairs[1:15:2] for p in ((i, j), (j, i))]),
    ]


def exchanged(pieces, axes):
    return lax.all_to_all(pieces, axes, 0, 0, tiled=True)


def summed(pieces, count, kind):
    (out,) = call(
        sum_kernel, [VM], [(VM, (count, 64, 128), kind)], flops=pieces.size, moved=4 * pieces.size
    )(pieces)
    return out


def in_hbm(*values):
    return [pltpu.with_memory_space_constraint(value, pltpu.HBM) for value in values]


def on_device(features, occupancy, weights, grad_out, lat_src, down_src, up_src, send_faces):
    sends = send_faces.transpose(0, 2, 1)
    masked, own, *out = call(
        faces_kernel, [HB] * 3, [(VM, BLOCKS, BF16)] + FACE_OUTS,
        [FEAT, OCC, PF, SEND, FACES_Z, pltpu.SemaphoreType.DMA((3,))],
    )(*in_hbm(features, occupancy, sends))
    half = (VM, (HALF, 128), F32)
    layer_out, delta, keep, give = call(
        forward_kernel,
        [HB] * 7 + [VM] * 8,
        [(HB, BLOCKS, BF16), (VM, BLOCKS, BF16), half, half],
        SCRATCH
        + [FEAT, pltpu.VMEM((ROWS, 128), F32), pltpu.VMEM((2 * C, MAIN + NB * 128), BF16)],
        limit=VMEM_LIMIT,
    )(
        *in_hbm(features, occupancy, grad_out, weights, lat_src, down_src, up_src),
        masked,
        own,
        *exchange(*out),
    )
    out = call(
        delta_faces_kernel, [VM, HB], FACE_OUTS[1:],
        [pltpu.VMEM((16, C, 128), BF16), PF, SEND, FACES_Z, pltpu.SemaphoreType.DMA((1,))],
        flops=2 * 384 * 512 * 768, moved=2 * 10**6,
    )(delta, *in_hbm(sends))
    (delta_own,) = call(
        delta_own_kernel, [HB], [(HB, (16, C, 128), BF16, pltpu.HBM)],
        [FEAT, pltpu.VMEM((16, C, 128), BF16), PF, pltpu.SemaphoreType.DMA((2,))],
        flops=2 * 384 * 512 * 512, moved=2 * 10**6,
    )(*in_hbm(delta))
    other = lax.ppermute(give, "c", [(0, 1), (1, 0)])
    other, *out = lax.optimization_barrier((other, *out))
    halos = exchange(*out)
    part = keep + other
    part = exchanged(part.reshape(16, HALF // 16, 128), PLANE)
    part, halos[1], halos[2] = lax.optimization_barrier(
        (part, halos[1], halos[2])
    )
    part = exchanged(summed(part, 8, F32), COLUMN)
    part, delta_own, halos[0], halos[3], halos[4], halos[5] = lax.optimization_barrier(
        (part, delta_own, halos[0], halos[3], halos[4], halos[5])
    )
    part = exchanged(summed(part, 16, BF16), PLANE)
    (input_grad,) = call(
        backward_kernel,
        [HB] * 14,
        [(HB, BLOCKS, BF16)],
        SCRATCH + [FEAT, pltpu.VMEM((4, C, 128), BF16), pltpu.VMEM((2, 2, C, 128), BF16)],
        flops=5 * 10**9, moved=4 * 10**6, limit=VMEM_LIMIT,
    )(
        *in_hbm(occupancy, grad_out, weights, lat_src, down_src, up_src, delta, delta_own),
        *in_hbm(*halos),
    )
    mine, input_grad = lax.optimization_barrier((part.reshape(HALF, 128), input_grad))
    other = lax.ppermute(mine, "c", [(0, 1), (1, 0)])
    (weight_grad,) = call(
        unpack_kernel, [VM, VM], [(HB, (TAPS * C, C), F32)],
        [pltpu.VMEM((ROWS, 128), F32), pltpu.VMEM((TAPS * C, C), F32), pltpu.SemaphoreType.DMA((3,))],
    )(mine, other)
    return layer_out, input_grad, weight_grad.reshape(TAPS, C, C)


def solution(mesh):
    fine = Mesh(mesh.devices.reshape(4, 2, 2, 4, 4), EVERY)
    split = P(EVERY)
    return jax.shard_map(
        on_device,
        mesh=fine,
        in_specs=(split, split, P(), split, split, split, split, split),
        out_specs=(split, split, P()),
        check_vma=False,
    )
```
